128 devices in a mesh: row: 8 (over y_lo, x), col: 16 (over z, y_hi, core).
Axes of the slice: x: 4, y: 4 (y_hi: 2, y_lo: 2; y = y_hi * 2 + y_lo), z: 4, core: 2. Of those that a mesh axis runs over, the one named last changes fastest.
Arguments:
- block_x: float32 [2048, 1024], P(('row', 'col'))
- tile_values: bfloat16 [8, 16, 1024, 4096], P('row', 'col')
- row_block: int32 [8, 16, 1024], P('row', 'col'), may hold values from 0 to 127, as said below
- col_block: int32 [8, 16, 1024], P('row', 'col'), may hold values from 0 to 255
- tile_counts: int32 [8, 16], P('row', 'col'), may hold values from 64 to 1024, as said below
Outputs:
- residual: float32 [2048, 1024], P(('row', 'col'))
- residual_image: float32 [2048, 1024], P(('row', 'col'))
- gram_small: float32 [16, 16], replicated
The draws below stay inside these ranges and needn't reach their ends.
Inputs may be any that keep to these rules, and one draw needn't show every extreme that they name: In grid cell (r, c) the first 16 slots s hold row_block = r * 16 + s and col_block = c * 16 + s, the diagonal tiles of the cell's own vector blocks; slots at or past the count hold indices in range too. `tile_counts`: some grid cell uses all 1024 slots in every draw.
All inputs are finite; a program needn't handle non-finite values.
Results may differ from the reference program's by a relative error of at most 0.0096.
Values may be sent and summed in bfloat16 or wider, within the bound.
A program may use at most 128 MiB of HBM per device.

```python
import jax
import jax.numpy as jnp
from jax import lax

TILE = 64
K = 16
SEGB = 16
TILES_DEV = 1024
RB = 128
CB = 256
NB = 2048
N_ROW = 8
N_COL = 16


def draw_block_x(key, part):
    key = jax.random.fold_in(key, 5)
    subkeys = jax.random.split(key, 2)
    position = (lax.iota(jnp.float32, NB) / NB)[:, None, None]
    level = jnp.exp(jax.random.uniform(subkeys[0], (NB, 1, 1), jnp.float32, jnp.log(0.2), jnp.log(2.0)))
    ramp = jnp.power(3.0, position)
    values = jax.random.normal(subkeys[1], (NB, K, TILE), jnp.float32) * level * ramp
    return values.reshape(NB, K * TILE)


def draw_tile_values(key, part):
    key = jax.random.fold_in(key, 4)
    subkeys = jax.random.split(key, 2)
    full_shape = (N_ROW, N_COL, TILES_DEV, TILE, TILE)
    spread = (TILE * N_ROW * TILES_DEV * 0.3 / RB) ** (-0.5)
    offdiag = jax.random.normal(subkeys[0], full_shape, jnp.float32) * spread
    small_shape = (N_ROW, N_COL, TILES_DEV, 1, 1)
    row_pos = lax.broadcasted_iota(jnp.int32, small_shape, 0)
    col_pos = lax.broadcasted_iota(jnp.int32, small_shape, 1)
    slot_pos = lax.broadcasted_iota(jnp.int32, small_shape, 2)
    global_block = (row_pos * N_COL + col_pos) * SEGB + slot_pos
    position = global_block.astype(jnp.float32) / NB
    strength = (1.0 + 2.0 * jax.random.uniform(subkeys[1], (N_ROW, N_COL, TILES_DEV, 1, TILE), jnp.float32)) * (1.0 + 2.0 * position)
    identity = jnp.eye(TILE, dtype=jnp.float32)
    diagonal_part = jnp.where(slot_pos < SEGB, 1.0, 0.0) * identity * strength
    values = offdiag + diagonal_part
    return values.reshape(N_ROW, N_COL, TILES_DEV, TILE * TILE).astype(jnp.bfloat16)


def draw_row_block(key, part):
    key = jax.random.fold_in(key, 1)
    grid_shape = (N_ROW, N_COL, TILES_DEV)
    row_pos = lax.broadcasted_iota(jnp.int32, grid_shape, 0)
    slot_pos = lax.broadcasted_iota(jnp.int32, grid_shape, 2)
    random_rows = jax.random.randint(key, grid_shape, 0, RB, dtype=jnp.int32)
    return jnp.where(slot_pos < SEGB, row_pos * SEGB + slot_pos, random_rows)


def draw_col_block(key, part):
    key = jax.random.fold_in(key, 2)
    grid_shape = (N_ROW, N_COL, TILES_DEV)
    col_pos = lax.broadcasted_iota(jnp.int32, grid_shape, 1)
    slot_pos = lax.broadcasted_iota(jnp.int32, grid_shape, 2)
    random_cols = jax.random.randint(key, grid_shape, 0, CB, dtype=jnp.int32)
    return jnp.where(slot_pos < SEGB, col_pos * SEGB + slot_pos, random_cols)


def draw_tile_counts(key, part):
    key = jax.random.fold_in(key, 3)
    subkeys = jax.random.split(key, 3)
    floor_count = max(SEGB, TILES_DEV // 16)
    count_span = TILES_DEV - floor_count
    grid_shape = (N_ROW, N_COL)
    draw_one = jax.random.randint(subkeys[0], grid_shape, 0, count_span + 1, dtype=jnp.int32)
    draw_two = jax.random.randint(subkeys[1], grid_shape, 0, count_span + 1, dtype=jnp.int32)
    counts = floor_count + draw_one * draw_two // count_span
    chosen = jax.random.randint(subkeys[2], (), 0, N_ROW * N_COL, dtype=jnp.int32)
    position = lax.broadcasted_iota(jnp.int32, grid_shape, 0) * N_COL + lax.broadcasted_iota(jnp.int32, grid_shape, 1)
    return jnp.where(position == chosen, TILES_DEV, counts).astype(jnp.int32)


def setup_inputs(seed: int = 0) -> dict:
    streams_of = jax.random.split(jax.random.key(seed), 6)
    return {
        "block_x": draw_block_x(jax.random.fold_in(streams_of[5], 71), 0),
        "tile_values": draw_tile_values(jax.random.fold_in(streams_of[5], 71), 0),
        "row_block": draw_row_block(jax.random.fold_in(streams_of[5], 71), 0),
        "col_block": draw_col_block(jax.random.fold_in(streams_of[5], 71), 0),
        "tile_counts": draw_tile_counts(jax.random.fold_in(streams_of[5], 71), 0),
    }


def apply_tiles(vectors, tile_values, row_block, col_block, tile_counts, transpose):
    slot_pos = jnp.arange(TILES_DEV, dtype=jnp.int32)

    def one_device(accum, device):
        row_pos = (device // N_COL).astype(jnp.int32)
        col_pos = (device % N_COL).astype(jnp.int32)
        square = tile_values[row_pos, col_pos].reshape(TILES_DEV, TILE, TILE).astype(jnp.float32)
        local_rows = row_block[row_pos, col_pos].astype(jnp.int32)
        local_cols = col_block[row_pos, col_pos].astype(jnp.int32)
        global_rows = ((local_rows // SEGB * N_COL + col_pos) * SEGB + local_rows % SEGB).astype(jnp.int32)
        global_cols = (row_pos * CB + local_cols).astype(jnp.int32)
        live_mask = (slot_pos < tile_counts[row_pos, col_pos])[:, None, None]
        if transpose:
            source = vectors[global_rows].astype(jnp.float32)
            contrib = jnp.einsum('tki,tij->tkj', source, square)
            target = global_cols
        else:
            source = vectors[global_cols].astype(jnp.float32)
            contrib = jnp.einsum('tkj,tij->tki', source, square)
            target = global_rows
        contrib = jnp.where(live_mask, contrib, 0.0)
        return (accum.at[target].add(contrib), None)
    start = jnp.zeros((NB, K, TILE), jnp.float32)
    devices = jnp.arange(N_ROW * N_COL, dtype=jnp.int32)
    return lax.scan(one_device, start, devices)[0]

def apply_hamiltonian(vectors, tile_values, row_block, col_block, tile_counts):
    forward = apply_tiles(vectors, tile_values, row_block, col_block, tile_counts, False)
    backward = apply_tiles(vectors, tile_values, row_block, col_block, tile_counts, True)
    return forward + backward

def gram_of(left, right):
    return jnp.einsum('bkj,blj->kl', left, right, precision=lax.Precision.HIGHEST)

def reference(block_x, tile_values, row_block, col_block, tile_counts):
    vectors = block_x.reshape(NB, K, TILE)
    x_half = block_x.astype(jnp.bfloat16).reshape(NB, K, TILE)
    image = apply_hamiltonian(x_half, tile_values, row_block, col_block, tile_counts)
    norm_gram = gram_of(vectors, vectors)
    cross_gram = gram_of(image, vectors)
    lower_factor = jnp.linalg.cholesky(norm_gram)
    halfway = lax.linalg.triangular_solve(lower_factor, cross_gram.T, left_side=True, lower=True)
    coupling_t = lax.linalg.triangular_solve(lower_factor, halfway, left_side=True, lower=True, transpose_a=True)
    residual = image - jnp.einsum('lk,blj->bkj', coupling_t, vectors, precision=lax.Precision.HIGHEST)
    residual_half = residual.astype(jnp.bfloat16)
    residual_image = apply_hamiltonian(residual_half, tile_values, row_block, col_block, tile_counts)
    gram_small = gram_of(residual, residual_image) / (NB * TILE)
    return (residual.reshape(NB, K * TILE), residual_image.reshape(NB, K * TILE), gram_small)
```

```python
import functools

import jax
import jax.numpy as jnp
from jax import lax
from jax.experimental import pallas as pl
from jax.experimental.pallas import tpu as pltpu
from jax.sharding import PartitionSpec as P

F32 = jnp.float32
BF16 = jnp.bfloat16
TILE = 64
K = 16
SEGB = 16
SLOTS = 1024
GROUPS = SLOTS // 4
WIDTH = K * TILE
N_ROW = 8
N_COL = 16
RB = N_ROW * SEGB
CB = N_COL * SEGB
STAGE_PITCH = 136
Y_PITCH = 520
HIGHEST = lax.Precision.HIGHEST
NT = (((1,), (1,)), ((), ()))
NN = (((1,), (0,)), ((), ()))


def left_half(rows):
    return lax.broadcasted_iota(jnp.int32, (rows, 128), 1) < TILE


def swap_halves(value):
    return pltpu.roll(value, TILE, 1)


def lane_block(index):
    start = index * 128
    if not isinstance(index, int):
        start = pl.multiple_of(start, 128)
    return pl.ds(start, 128)


def flat_to_by_vector(flat, temp, out):
    lt = left_half(8)

    def step(pair, carry):
        low = flat[0:8, lane_block(pair)]
        high = flat[8:16, lane_block(pair)]
        temp[pl.ds(2 * pair, 8, stride=K), :] = jnp.where(lt, low, swap_halves(high))
        temp[pl.ds(2 * pair + 1, 8, stride=K), :] = jnp.where(lt, swap_halves(low), high)
        return carry

    lax.fori_loop(0, K // 2, step, 0, unroll=True)
    gather_blocks(temp, out)


def gather_blocks(temp, out):
    def step(p, carry):
        out[:, lane_block(p)] = temp[pl.ds(pl.multiple_of(p * K, K), K), :]
        return carry

    lax.fori_loop(0, 8, step, 0, unroll=True)


def by_row_to_by_vector(by_row, temp, out):
    def step(k, carry):
        temp[pl.ds(k, 8, stride=K), :] = by_row[pl.ds(pl.multiple_of(k * 8, 8), 8), :]
        return carry

    lax.fori_loop(0, K, step, 0, unroll=True)
    gather_blocks(temp, out)


def by_vector_to_by_row(by_vector, temp, out):
    def spread(p, carry):
        temp[pl.ds(pl.multiple_of(p * K, K), K), :] = by_vector[:, lane_block(p)]
        return carry

    def collect(k, carry):
        out[pl.ds(pl.multiple_of(k * 8, 8), 8), :] = temp[pl.ds(k, 8, stride=K), :]
        return carry

    lax.fori_loop(0, 8, spread, 0, unroll=True)
    lax.fori_loop(0, K, collect, 0, unroll=True)


def by_row_to_flat(by_row, flat):
    lt = left_half(8)

    def step(pair, carry):
        even = by_row[pl.ds(pl.multiple_of(pair * 16, 8), 8), :]
        odd = by_row[pl.ds(pl.multiple_of(pair * 16 + 8, 8), 8), :]
        flat[0:8, lane_block(pair)] = jnp.where(lt, even, swap_halves(odd))
        flat[8:16, lane_block(pair)] = jnp.where(lt, swap_halves(even), odd)
        return carry

    lax.fori_loop(0, K // 2, step, 0, unroll=True)


def load_groups(raw, stage, tiles, chunk, count):
    lt = left_half(16)
    lane_row = lax.broadcasted_iota(jnp.int32, (16, 128), 0)

    def half(a, carry):
        live = [lane_row + ((2 * a + b) * GROUPS + chunk * 16) < count for b in range(2)]

        def step(m, inner):
            first = jnp.where(live[0], raw[chunk, 2 * a, :, lane_block(m)].astype(F32), 0.0)
            second = jnp.where(live[1], raw[chunk, 2 * a + 1, :, lane_block(m)].astype(F32), 0.0)
            even = jnp.where(lt, first, swap_halves(second))
            odd = jnp.where(lt, swap_halves(first), second)
            for h in range(2):
                base = h * 8 * STAGE_PITCH + a * TILE + 2 * m
                stage[pl.ds(base, 8, stride=STAGE_PITCH), :] = even[h * 8 : h * 8 + 8]
                stage[pl.ds(base + 1, 8, stride=STAGE_PITCH), :] = odd[h * 8 : h * 8 + 8]
            return inner

        return lax.fori_loop(0, 32, step, carry, unroll=True)

    lax.fori_loop(0, 2, half, 0, unroll=True)

    def narrow(u, carry):
        tiles[chunk * 16 + u] = stage[pl.ds(pl.multiple_of(u * STAGE_PITCH, 8), 128), :].astype(BF16)
        return carry

    lax.fori_loop(0, 16, narrow, 0, unroll=True)


def fill_table(own, table, base):
    lt = left_half(16)
    zero = jnp.zeros((16, 128), BF16)

    def step(p, carry):
        both = own[:, lane_block(p)]
        turned = swap_halves(both)
        table[base + p, 0] = jnp.where(lt, both, zero)
        table[base + p, 1] = jnp.where(lt, zero, turned)
        table[base + 8 + p, 0] = jnp.where(lt, turned, zero)
        table[base + 8 + p, 1] = jnp.where(lt, zero, both)
        return carry

    lax.fori_loop(0, 8, step, 0, unroll=True)


def multiply(index, table, tiles, products, forward, turned=None):
    lt = left_half(16)

    def step(q, carry):
        picked = [table[index[0, 0, g * GROUPS + q], (g % 2) if forward else (g // 2)] for g in range(4)]
        left = jnp.concatenate(picked, axis=0)
        matrix = tiles[q]
        if turned is not None:
            turned[q] = matrix.T
        out = lax.dot_general(left, matrix, NN, preferred_element_type=F32)
        for s in range(2):
            one, two = (s, 2 + s) if forward else (2 * s, 2 * s + 1)
            merged = jnp.where(lt, out[one * 16 : one * 16 + 16], out[two * 16 : two * 16 + 16])
            place = s * GROUPS + q
            products[pl.ds(place, 8, stride=Y_PITCH), :] = merged[:8]
            products[pl.ds(8 * Y_PITCH + place, 8, stride=Y_PITCH), :] = merged[8:]
        return carry

    lax.fori_loop(0, GROUPS, step, 0, unroll=64)


def add_up(places, products, out, blocks):
    lt = left_half(8)

    def step(pair, carry):
        part = [
            products[pl.ds(pl.multiple_of((2 * pair + i) * Y_PITCH, 8), SLOTS // 2), :].astype(BF16) for i in range(2)
        ]
        total = jnp.dot(places[...], jnp.concatenate(part, axis=1), preferred_element_type=F32)
        for target in range(blocks // SEGB):
            rows = []
            for i in range(2):
                half = []
                for h in range(2):
                    first = target * SEGB + h * 8
                    left = total[first : first + 8, i * 128 : i * 128 + 128]
                    right = total[blocks + first : blocks + first + 8, i * 128 : i * 128 + 128]
                    both = jnp.where(lt, left, right)
                    half.append(both + swap_halves(both))
                rows.append(jnp.where(lt, half[0], half[1]))
            out[target, pl.ds(pl.multiple_of(pair * 16, 16), 16), :] = jnp.concatenate(rows, axis=0).astype(BF16)
        return carry

    lax.fori_loop(0, K // 2, step, 0, unroll=True)


def factor(norm):
    row = lax.broadcasted_iota(jnp.int32, (K, K), 0)
    lane = lax.broadcasted_iota(jnp.int32, (K, K), 1)

    def step(j, carry):
        matrix, inverse = carry
        pivot_row = jnp.sum(jnp.where(row == j, matrix, 0.0), axis=0, keepdims=True)
        pivot_inv = jnp.sum(jnp.where(row == j, inverse, 0.0), axis=0, keepdims=True)
        column = jnp.sum(jnp.where(lane == j, matrix, 0.0), axis=1, keepdims=True)
        pivot = jnp.sum(jnp.where((lane == j) & (row == j), matrix, 0.0), keepdims=True)
        scale = jnp.where(row[:, 0:1] > j, column / pivot, 0.0)
        return matrix - scale * pivot_row, inverse - scale * pivot_inv

    start = (norm, jnp.where(row == lane, 1.0, 0.0).astype(F32))
    matrix, inverse = lax.fori_loop(0, K, step, start)
    diagonal = jnp.sum(jnp.where(row == lane, matrix, 0.0), axis=1, keepdims=True)
    return inverse, 1.0 / diagonal


def kernel(
    block_x, tile_values, row_s, col_s, count_s, row_v, col_v,
    residual_out, image_out, gram_out,
    raw, stage, tiles, turned, table_r, table_c, place_r, place_c, prod_r, prod_c,
    temp, by_row, vec_x, vec_a, vec_b, own, got_r, got_c, part_r, part_c, sum_r, sum_c, gram_own, gram_r, gram_c,
    load_sem, send_r, send_c, recv_r, recv_c,
):
    my_row, my_col = lax.axis_index("row"), lax.axis_index("col")
    axes = {"row": (N_ROW, my_row, send_r, recv_r), "col": (N_COL, my_col, send_c, recv_c)}

    def copy(axis, kind, source, target, slot, peer):
        size, me, send, recv = axes[axis]
        return pltpu.make_async_remote_copy(
            src_ref=source, dst_ref=target, send_sem=send.at[kind, peer], recv_sem=recv.at[kind, slot],
            device_id={axis: peer}, device_id_type=pl.DeviceIdType.MESH,
        )

    def send_all(axis, kind, source_of, buffer):
        size, me, _, _ = axes[axis]

        def step(d, carry):
            peer = lax.rem(me + d, size)
            copy(axis, kind, source_of(peer), buffer.at[me], me, peer).start()
            return carry

        lax.fori_loop(1, size, step, 0)

    def finish_sends(axis, kind, source_of, buffer):
        size, me, _, _ = axes[axis]

        def step(d, carry):
            peer = lax.rem(me + d, size)
            copy(axis, kind, source_of(peer), buffer.at[me], me, peer).wait_send()
            return carry

        lax.fori_loop(1, size, step, 0)

    def each_arrival(axis, kind, source_of, buffer, use, start=0):
        size, me, _, _ = axes[axis]

        def step(d, carry):
            slot = lax.rem(me + size - d, size)
            copy(axis, kind, source_of(slot), buffer.at[slot], slot, slot).wait_recv()
            return use(slot, carry)

        return lax.fori_loop(1, size, step, start)

    def load(chunk, g):
        return pltpu.make_async_copy(
            tile_values.at[0, 0, pl.ds(pl.multiple_of(g * GROUPS + chunk * 16, 16), 16), :],
            raw.at[chunk, g], load_sem.at[chunk, g],
        )

    def start_load(chunk, carry):
        for g in range(4):
            load(chunk, g).start()
        return carry

    lax.fori_loop(0, SLOTS // 64, start_load, 0)
    barrier = pltpu.get_barrier_semaphore()
    for axis in ("row", "col"):
        size, me, _, _ = axes[axis]

        def greet(d, carry, axis=axis, size=size, me=me):
            pl.semaphore_signal(
                barrier, inc=1, device_id={axis: lax.rem(me + d, size)}, device_id_type=pl.DeviceIdType.MESH
            )
            return carry

        lax.fori_loop(1, size, greet, 0)

    flat_to_by_vector(block_x, temp, vec_x)
    own[0] = vec_x[...].astype(BF16)
    norm = lax.dot_general(vec_x[...], vec_x[...], NT, precision=HIGHEST, preferred_element_type=F32)
    gram_own[0] = jnp.zeros((K, 128), F32)
    gram_own[0, :, 0:K] = norm

    pl.semaphore_wait(barrier, N_ROW + N_COL - 2)

    def gather(step):
        source = lambda peer: own.at[step]
        send_all("row", step, source, got_r.at[step])
        send_all("col", step, source, got_c.at[step])

    def gram_row(which):
        source = lambda peer: gram_own.at[which]
        send_all("row", 4 + which, source, gram_r.at[which])
        gram_r[which, my_row] = gram_own[which]

    def gram_col(which):
        each_arrival("row", 4 + which, lambda s: gram_own.at[which], gram_r.at[which], lambda s, c: c)
        gram_own[3 + which] = jnp.sum(gram_r[which], axis=0)
        source = lambda peer: gram_own.at[3 + which]
        send_all("col", 4 + which, source, gram_c.at[which])
        gram_c[which, my_col] = gram_own[3 + which]

    def gram_done(which):
        each_arrival("col", 4 + which, lambda s: gram_own.at[3 + which], gram_c.at[which], lambda s, c: c)
        return jnp.sum(gram_c[which], axis=0)[:, 0:K]

    gather(0)
    gram_row(0)

    count = count_s[0, 0]

    def arrange(chunk, carry):
        for g in range(4):
            load(chunk, g).wait()
        load_groups(raw, stage, tiles, chunk, count)
        return carry

    lax.fori_loop(0, SLOTS // 64, arrange, 0)
    for s in range(2):
        columns = jnp.concatenate(
            [col_v[0, :, s * 256 : s * 256 + 256], col_v[0, :, 512 + s * 256 : 768 + s * 256]], axis=1
        )
        hit = lax.broadcasted_iota(jnp.int32, (CB, 512), 0) == columns
        place_c[s * CB : s * CB + CB, :] = jnp.where(hit, 1.0, 0.0).astype(BF16)
        hit = lax.broadcasted_iota(jnp.int32, (RB, 512), 0) == row_v[0, :, s * 512 : s * 512 + 512]
        place_r[s * RB : s * RB + RB, :] = jnp.where(hit, 1.0, 0.0).astype(BF16)
    gram_col(0)

    def product(step, while_waiting):
        source = lambda s: own.at[step]

        def enter(buffer, table):
            def use(slot, carry):
                fill_table(buffer.at[step, slot], table, slot * SEGB)
                return carry

            return use

        fill_table(own.at[step], table_r, my_row * SEGB)
        each_arrival("row", step, source, got_r.at[step], enter(got_r, table_r))
        multiply(row_s, table_r, tiles, prod_c, False, turned if step == 0 else None)
        add_up(place_c, prod_c, part_c.at[step], CB)
        send_all("col", 2 + step, lambda peer: part_c.at[step, peer], sum_c.at[step])
        fill_table(own.at[step], table_c, my_col * SEGB)
        each_arrival("col", step, source, got_c.at[step], enter(got_c, table_c))
        multiply(col_s, table_c, turned, prod_r, True)
        add_up(place_r, prod_r, part_r.at[step], RB)
        send_all("row", 2 + step, lambda peer: part_r.at[step, peer], sum_r.at[step])
        extra = while_waiting()
        total = part_c[step, my_col].astype(F32) + part_r[step, my_row].astype(F32)

        def add(buffer):
            return lambda slot, carry: carry + buffer[step, slot].astype(F32)

        total = each_arrival("col", 2 + step, lambda s: part_c.at[step, s], sum_c.at[step], add(sum_c), total)
        total = each_arrival("row", 2 + step, lambda s: part_r.at[step, s], sum_r.at[step], add(sum_r), total)
        by_row[...] = total
        return extra

    inverse, scale = product(0, lambda: factor(gram_done(0)))
    by_row_to_by_vector(by_row, temp, vec_a)
    gram_own[1] = jnp.zeros((K, 128), F32)
    gram_own[1, :, 0:K] = lax.dot_general(vec_a[...], vec_x[...], NT, precision=HIGHEST, preferred_element_type=F32)
    gram_row(1)
    gram_col(1)
    cross = gram_done(1)
    halfway = lax.dot_general(inverse, cross, NT, precision=HIGHEST, preferred_element_type=F32) * scale
    coupling = lax.dot_general(
        halfway, inverse, (((0,), (0,)), ((), ())), precision=HIGHEST, preferred_element_type=F32
    )
    vec_a[...] = vec_a[...] - jnp.dot(coupling, vec_x[...], precision=HIGHEST, preferred_element_type=F32)
    own[1] = vec_a[...].astype(BF16)
    gather(1)
    by_vector_to_by_row(vec_a, temp, by_row)
    by_row_to_flat(by_row, residual_out)

    product(1, lambda: None)
    by_row_to_by_vector(by_row, temp, vec_b)
    gram_own[2] = jnp.zeros((K, 128), F32)
    gram_own[2, :, 0:K] = lax.dot_general(vec_a[...], vec_b[...], NT, precision=HIGHEST, preferred_element_type=F32)
    gram_row(2)
    by_row_to_flat(by_row, image_out)
    gram_col(2)
    gram_out[...] = gram_done(2) * (1.0 / (N_ROW * N_COL * SEGB * TILE))

    for step in range(2):
        source = lambda peer, step=step: own.at[step]
        finish_sends("row", step, source, got_r.at[step])
        finish_sends("col", step, source, got_c.at[step])
        finish_sends("row", 2 + step, lambda peer, step=step: part_r.at[step, peer], sum_r.at[step])
        finish_sends("col", 2 + step, lambda peer, step=step: part_c.at[step, peer], sum_c.at[step])
    for which in range(3):
        finish_sends("row", 4 + which, lambda peer, which=which: gram_own.at[which], gram_r.at[which])
        finish_sends("col", 4 + which, lambda peer, which=which: gram_own.at[3 + which], gram_c.at[which])


def local(block_x, tile_values, row_block, col_block, tile_counts):
    vmem = pl.BlockSpec(memory_space=pltpu.VMEM)
    smem = pl.BlockSpec(memory_space=pltpu.SMEM)
    kinds = 7
    return pl.pallas_call(
        kernel,
        out_shape=(
            jax.ShapeDtypeStruct((SEGB, WIDTH), F32),
            jax.ShapeDtypeStruct((SEGB, WIDTH), F32),
            jax.ShapeDtypeStruct((K, K), F32),
        ),
        in_specs=[vmem, pl.BlockSpec(memory_space=pl.ANY), smem, smem, smem, vmem, vmem],
        out_specs=(vmem, vmem, vmem),
        scratch_shapes=[
            pltpu.VMEM((SLOTS // 64, 4, 16, TILE * TILE), BF16),
            pltpu.VMEM((16 * STAGE_PITCH, 128), F32),
            pltpu.VMEM((GROUPS, 128, 128), BF16),
            pltpu.VMEM((GROUPS, 128, 128), BF16),
            pltpu.VMEM((RB, 2, K, 128), BF16),
            pltpu.VMEM((CB, 2, K, 128), BF16),
            pltpu.VMEM((2 * RB, 512), BF16),
            pltpu.VMEM((2 * CB, 512), BF16),
            pltpu.VMEM((K * Y_PITCH, 128), F32),
            pltpu.VMEM((K * Y_PITCH, 128), F32),
            pltpu.VMEM((128, 128), F32),
            pltpu.VMEM((128, 128), F32),
            pltpu.VMEM((K, WIDTH), F32),
            pltpu.VMEM((K, WIDTH), F32),
            pltpu.VMEM((K, WIDTH), F32),
            pltpu.VMEM((2, K, WIDTH), BF16),
            pltpu.VMEM((2, N_ROW, K, WIDTH), BF16),
            pltpu.VMEM((2, N_COL, K, WIDTH), BF16),
            pltpu.VMEM((2, N_ROW, 128, 128), BF16),
            pltpu.VMEM((2, N_COL, 128, 128), BF16),
            pltpu.VMEM((2, N_ROW, 128, 128), BF16),
            pltpu.VMEM((2, N_COL, 128, 128), BF16),
            pltpu.VMEM((6, K, 128), F32),
            pltpu.VMEM((3, N_ROW, K, 128), F32),
            pltpu.VMEM((3, N_COL, K, 128), F32),
            pltpu.SemaphoreType.DMA((SLOTS // 64, 4)),
            pltpu.SemaphoreType.DMA((kinds, N_ROW)),
            pltpu.SemaphoreType.DMA((kinds, N_COL)),
            pltpu.SemaphoreType.DMA((kinds, N_ROW)),
            pltpu.SemaphoreType.DMA((kinds, N_COL)),
        ],
        compiler_params=pltpu.CompilerParams(
            collective_id=0, has_side_effects=True, vmem_limit_bytes=58 << 20
        ),
        cost_estimate=pl.CostEstimate(flops=1 << 30, bytes_accessed=9 << 20, transcendentals=0),
    )(block_x, tile_values, row_block, col_block, tile_counts, row_block, col_block)


def solution(mesh):
    placed = (
        P(("row", "col"), None),
        P("row", "col", None, None),
        P("row", "col", None),
        P("row", "col", None),
        P("row", "col"),
    )
    return jax.shard_map(
        local,
        mesh=mesh,
        in_specs=placed,
        out_specs=(P(("row", "col"), None), P(("row", "col"), None), P()),
        check_vma=False,
    )
```

```python
import functools

import jax
import jax.numpy as jnp
from jax import lax
from jax.experimental import pallas as pl
from jax.experimental.pallas import tpu as pltpu
from jax.sharding import PartitionSpec as P

F32 = jnp.float32
BF16 = jnp.bfloat16
TILE = 64
K = 16
SEGB = 16
SLOTS = 1024
GROUPS = SLOTS // 4
WIDTH = K * TILE
N_ROW = 8
N_COL = 16
RB = N_ROW * SEGB
CB = N_COL * SEGB
STAGE_PITCH = 136
Y_PITCH = 520
EARLY_CHUNKS = 8
HIGHEST = lax.Precision.HIGHEST
NT = (((1,), (1,)), ((), ()))
NN = (((1,), (0,)), ((), ()))


def left_half(rows):
    return lax.broadcasted_iota(jnp.int32, (rows, 128), 1) < TILE


def swap_halves(value):
    return pltpu.roll(value, TILE, 1)


def lane_block(index):
    start = index * 128
    if not isinstance(index, int):
        start = pl.multiple_of(start, 128)
    return pl.ds(start, 128)


def flat_to_by_vector(flat, temp, out):
    lt = left_half(8)

    def step(pair, carry):
        low = flat[0:8, lane_block(pair)]
        high = flat[8:16, lane_block(pair)]
        temp[pl.ds(2 * pair, 8, stride=K), :] = jnp.where(lt, low, swap_halves(high))
        temp[pl.ds(2 * pair + 1, 8, stride=K), :] = jnp.where(lt, swap_halves(low), high)
        return carry

    lax.fori_loop(0, K // 2, step, 0, unroll=True)
    gather_blocks(temp, out)


def gather_blocks(temp, out):
    def step(p, carry):
        out[:, lane_block(p)] = temp[pl.ds(pl.multiple_of(p * K, K), K), :]
        return carry

    lax.fori_loop(0, 8, step, 0, unroll=True)


def by_vector_to_by_row(by_vector, temp, out):
    def spread(p, carry):
        temp[pl.ds(pl.multiple_of(p * K, K), K), :] = by_vector[:, lane_block(p)]
        return carry

    def collect(k, carry):
        out[pl.ds(pl.multiple_of(k * 8, 8), 8), :] = temp[pl.ds(k, 8, stride=K), :]
        return carry

    lax.fori_loop(0, 8, spread, 0, unroll=True)
    lax.fori_loop(0, K, collect, 0, unroll=True)


def by_row_to_flat(by_row, flat):
    lt = left_half(8)

    def step(pair, carry):
        even = by_row[pl.ds(pl.multiple_of(pair * 16, 8), 8), :]
        odd = by_row[pl.ds(pl.multiple_of(pair * 16 + 8, 8), 8), :]
        flat[0:8, lane_block(pair)] = jnp.where(lt, even, swap_halves(odd))
        flat[8:16, lane_block(pair)] = jnp.where(lt, swap_halves(even), odd)
        return carry

    lax.fori_loop(0, K // 2, step, 0, unroll=True)


def load_groups(raw, stage, tiles, chunk, count):
    lt = left_half(16)
    lane_row = lax.broadcasted_iota(jnp.int32, (16, 128), 0)

    def half(a, carry):
        live = [lane_row + ((2 * a + b) * GROUPS + chunk * 16) < count for b in range(2)]

        def step(m, inner):
            first = jnp.where(live[0], raw[chunk, 2 * a, :, lane_block(m)].astype(F32), 0.0)
            second = jnp.where(live[1], raw[chunk, 2 * a + 1, :, lane_block(m)].astype(F32), 0.0)
            even = jnp.where(lt, first, swap_halves(second))
            odd = jnp.where(lt, swap_halves(first), second)
            for h in range(2):
                base = h * 8 * STAGE_PITCH + a * TILE + 2 * m
                stage[pl.ds(base, 8, stride=STAGE_PITCH), :] = even[h * 8 : h * 8 + 8]
                stage[pl.ds(base + 1, 8, stride=STAGE_PITCH), :] = odd[h * 8 : h * 8 + 8]
            return inner

        return lax.fori_loop(0, 32, step, carry, unroll=True)

    lax.fori_loop(0, 2, half, 0, unroll=True)

    def narrow(u, carry):
        tiles[chunk * 16 + u] = stage[pl.ds(pl.multiple_of(u * STAGE_PITCH, 8), 128), :].astype(BF16)
        return carry

    lax.fori_loop(0, 16, narrow, 0, unroll=True)


def fill_table(own, table, base):
    lt = left_half(16)
    zero = jnp.zeros((16, 128), BF16)

    def step(p, carry):
        both = own[:, lane_block(p)]
        turned = swap_halves(both)
        table[base + p, 0] = jnp.where(lt, both, zero)
        table[base + p, 1] = jnp.where(lt, zero, turned)
        table[base + 8 + p, 0] = jnp.where(lt, turned, zero)
        table[base + 8 + p, 1] = jnp.where(lt, zero, both)
        return carry

    lax.fori_loop(0, 8, step, 0, unroll=True)


def multiply(index, table, tiles, products, forward, turned=None):
    lt = left_half(16)

    def step(q, carry):
        picked = [table[index[0, 0, g * GROUPS + q], (g % 2) if forward else (g // 2)] for g in range(4)]
        left = jnp.concatenate(picked, axis=0)
        matrix = tiles[q]
        if turned is not None:
            turned[q] = matrix.T
        out = lax.dot_general(left, matrix, NN, preferred_element_type=F32)
        for s in range(2):
            one, two = (s, 2 + s) if forward else (2 * s, 2 * s + 1)
            merged = jnp.where(lt, out[one * 16 : one * 16 + 16], out[two * 16 : two * 16 + 16])
            place = s * GROUPS + q
            products[pl.ds(place, 8, stride=Y_PITCH), :] = merged[:8]
            products[pl.ds(8 * Y_PITCH + place, 8, stride=Y_PITCH), :] = merged[8:]
        return carry

    lax.fori_loop(0, GROUPS, step, 0, unroll=64)


def add_up(places, products, temp, out, blocks):
    lt = left_half(8)
    targets = blocks // SEGB

    def step(pair, carry):
        part = [
            products[pl.ds(pl.multiple_of((2 * pair + i) * Y_PITCH, 8), SLOTS // 2), :].astype(BF16) for i in range(2)
        ]
        total = jnp.dot(places[...], jnp.concatenate(part, axis=1), preferred_element_type=F32)
        for target in range(targets):
            for i in range(2):
                half = []
                for h in range(2):
                    first = target * SEGB + h * 8
                    left = total[first : first + 8, i * 128 : i * 128 + 128]
                    right = total[blocks + first : blocks + first + 8, i * 128 : i * 128 + 128]
                    both = jnp.where(lt, left, right)
                    half.append(both + swap_halves(both))
                temp[pl.ds(target * 128 + 2 * pair + i, 8, stride=K), :] = jnp.where(lt, half[0], half[1])
        return carry

    lax.fori_loop(0, K // 2, step, 0, unroll=True)

    def narrow(target, carry):
        for p in range(8):
            rows = pl.ds(pl.multiple_of(target * 128 + p * K, K), K)
            out[target, :, p * 128 : p * 128 + 128] = temp[rows, :].astype(BF16)
        return carry

    lax.fori_loop(0, targets, narrow, 0, unroll=True)


def factor(norm):
    row = lax.broadcasted_iota(jnp.int32, (K, K), 0)
    lane = lax.broadcasted_iota(jnp.int32, (K, K), 1)

    def step(j, carry):
        matrix, inverse = carry
        pivot_row = jnp.sum(jnp.where(row == j, matrix, 0.0), axis=0, keepdims=True)
        pivot_inv = jnp.sum(jnp.where(row == j, inverse, 0.0), axis=0, keepdims=True)
        column = jnp.sum(jnp.where(lane == j, matrix, 0.0), axis=1, keepdims=True)
        pivot = jnp.sum(jnp.where((lane == j) & (row == j), matrix, 0.0), keepdims=True)
        scale = jnp.where(row[:, 0:1] > j, column / pivot, 0.0)
        return matrix - scale * pivot_row, inverse - scale * pivot_inv

    start = (norm, jnp.where(row == lane, 1.0, 0.0).astype(F32))
    matrix, inverse = lax.fori_loop(0, K, step, start)
    diagonal = jnp.sum(jnp.where(row == lane, matrix, 0.0), axis=1, keepdims=True)
    return inverse, 1.0 / diagonal


def kernel(
    block_x, tile_values, row_s, col_s, count_s, row_v, col_v,
    residual_out, image_out, gram_out,
    raw, stage, tiles, turned, table_r, table_c, place_r, place_c, prod_r, prod_c,
    temp, vec_x, vec_a, own, got_r, got_c, part_r, part_c, sum_r, sum_c, gram_own, gram_r, gram_c,
    load_sem, send_r, send_c, recv_r, recv_c, gram_recv_r, gram_recv_c,
):
    my_row, my_col = lax.axis_index("row"), lax.axis_index("col")
    size_of = {"row": N_ROW, "col": N_COL}
    me_of = {"row": my_row, "col": my_col}
    send_of = {"row": send_r, "col": send_c}
    recv_of = {"row": recv_r, "col": recv_c}
    gram_recv_of = {"row": gram_recv_r, "col": gram_recv_c}

    def send_all(axis, kind, source_of, buffer):
        size, me = size_of[axis], me_of[axis]
        arrived = recv_of[axis].at[kind, me] if kind < 4 else gram_recv_of[axis].at[kind - 4]

        def step(d, carry):
            peer = lax.rem(me + d, size)
            pltpu.make_async_remote_copy(
                src_ref=source_of(peer), dst_ref=buffer.at[me], send_sem=send_of[axis].at[kind], recv_sem=arrived,
                device_id={axis: peer}, device_id_type=pl.DeviceIdType.MESH,
            ).start()
            return carry

        lax.fori_loop(1, size, step, 0)

    def wait_bytes(buffer, axis, sem):
        block = buffer.at[pl.ds(0, size_of[axis] - 1)]
        pltpu.make_async_copy(block, block, sem).wait()

    def each_arrival(axis, kind, buffer, use, start=0):
        size, me = size_of[axis], me_of[axis]

        def step(d, carry):
            slot = lax.rem(me + size - d, size)
            pltpu.make_async_copy(buffer.at[slot], buffer.at[slot], recv_of[axis].at[kind, slot]).wait()
            return use(slot, carry)

        return lax.fori_loop(1, size, step, start)

    def load(chunk, g):
        return pltpu.make_async_copy(
            tile_values.at[0, 0, pl.ds(pl.multiple_of(g * GROUPS + chunk * 16, 16), 16), :],
            raw.at[chunk, g], load_sem.at[chunk, g],
        )

    def start_load(chunk, carry):
        for g in range(4):
            load(chunk, g).start()
        return carry

    barrier = pltpu.get_barrier_semaphore()
    for axis in ("row", "col"):

        def greet(d, carry, axis=axis):
            pl.semaphore_signal(
                barrier, inc=1, device_id={axis: lax.rem(me_of[axis] + d, size_of[axis])},
                device_id_type=pl.DeviceIdType.MESH,
            )
            return carry

        lax.fori_loop(1, size_of[axis], greet, 0)

    lax.fori_loop(0, SLOTS // 64, start_load, 0)
    flat_to_by_vector(block_x, temp, vec_x)
    own[0] = vec_x[...].astype(BF16)
    norm = lax.dot_general(vec_x[...], vec_x[...], NT, precision=HIGHEST, preferred_element_type=F32)
    gram_own[0] = jnp.zeros((K, 128), F32)
    gram_own[0, :, 0:K] = norm
    count = count_s[0, 0]

    def arrange(chunk, carry):
        for g in range(4):
            load(chunk, g).wait()
        load_groups(raw, stage, tiles, chunk, count)
        return carry

    lax.fori_loop(0, EARLY_CHUNKS, arrange, 0)
    pl.semaphore_wait(barrier, N_ROW + N_COL - 2)

    def gather(step):
        send_all("row", step, lambda peer: own.at[step], got_r.at[step])
        send_all("col", step, lambda peer: own.at[step], got_c.at[step])

    def gram_row(which):
        send_all("row", 4 + which, lambda peer: gram_own.at[which], gram_r.at[which])
        gram_r[which, my_row] = gram_own[which]

    def gram_col(which):
        wait_bytes(gram_r.at[which], "row", gram_recv_r.at[which])
        gram_own[3 + which] = jnp.sum(gram_r[which], axis=0)
        send_all("col", 4 + which, lambda peer: gram_own.at[3 + which], gram_c.at[which])
        gram_c[which, my_col] = gram_own[3 + which]

    def gram_done(which):
        wait_bytes(gram_c.at[which], "col", gram_recv_c.at[which])
        return jnp.sum(gram_c[which], axis=0)[:, 0:K]

    def cross_part(step):
        def dot(slot, carry):
            return carry + lax.dot_general(part_c[step, slot], got_c[step, slot], NT, preferred_element_type=F32)

        return lax.fori_loop(0, N_COL, dot, jnp.zeros((K, K), F32), unroll=True)

    def finish_sends(step):
        wait_bytes(got_r.at[step], "row", send_r.at[step])
        wait_bytes(got_c.at[step], "col", send_c.at[step])
        wait_bytes(part_r.at[step], "row", send_r.at[2 + step])
        wait_bytes(part_c.at[step], "col", send_c.at[2 + step])
        for which in (0, 1) if step == 0 else (2,):
            wait_bytes(gram_r.at[which], "row", send_r.at[4 + which])
            wait_bytes(gram_c.at[which], "col", send_c.at[4 + which])

    gather(0)
    gram_row(0)
    lax.fori_loop(EARLY_CHUNKS, SLOTS // 64, arrange, 0)
    for s in range(2):
        columns = jnp.concatenate(
            [col_v[0, :, s * 256 : s * 256 + 256], col_v[0, :, 512 + s * 256 : 768 + s * 256]], axis=1
        )
        hit = lax.broadcasted_iota(jnp.int32, (CB, 512), 0) == columns
        place_c[s * CB : s * CB + CB, :] = jnp.where(hit, 1.0, 0.0).astype(BF16)
        hit = lax.broadcasted_iota(jnp.int32, (RB, 512), 0) == row_v[0, :, s * 512 : s * 512 + 512]
        place_r[s * RB : s * RB + RB, :] = jnp.where(hit, 1.0, 0.0).astype(BF16)
    gram_col(0)

    def product(step, while_waiting):
        def enter(buffer, table):
            def use(slot, carry):
                fill_table(buffer.at[step, slot], table, slot * SEGB)
                return carry

            return use

        fill_table(own.at[step], table_r, my_row * SEGB)
        each_arrival("row", step, got_r.at[step], enter(got_r, table_r))
        multiply(row_s, table_r, tiles, prod_c, False, turned if step == 0 else None)
        add_up(place_c, prod_c, temp, part_c.at[step], CB)
        send_all("col", 2 + step, lambda peer: part_c.at[step, peer], sum_c.at[step])
        fill_table(own.at[step], table_c, my_col * SEGB)
        got_c[step, my_col] = own[step]
        each_arrival("col", step, got_c.at[step], enter(got_c, table_c))
        gram_own[1 + step] = jnp.zeros((K, 128), F32)
        gram_own[1 + step, :, 0:K] = cross_part(step)
        gram_row(1 + step)
        multiply(col_s, table_c, turned, prod_r, True)
        add_up(place_r, prod_r, temp, part_r.at[step], RB)
        send_all("row", 2 + step, lambda peer: part_r.at[step, peer], sum_r.at[step])
        gram_col(1 + step)
        extra = while_waiting()
        vec_a[...] = part_c[step, my_col].astype(F32) + part_r[step, my_row].astype(F32)

        def add(buffer):
            def use(slot, carry):
                vec_a[...] += buffer[step, slot].astype(F32)
                return carry

            return use

        each_arrival("col", 2 + step, sum_c.at[step], add(sum_c))
        each_arrival("row", 2 + step, sum_r.at[step], add(sum_r))
        half = gram_done(1 + step)
        return half + half.T, extra

    cross, (inverse, scale) = product(0, lambda: factor(gram_done(0)))
    halfway = lax.dot_general(inverse, cross, NT, precision=HIGHEST, preferred_element_type=F32) * scale
    coupling = lax.dot_general(
        halfway, inverse, (((0,), (0,)), ((), ())), precision=HIGHEST, preferred_element_type=F32
    )
    residual = vec_a[...] - jnp.dot(coupling, vec_x[...], precision=HIGHEST, preferred_element_type=F32)
    own[1] = residual.astype(BF16)
    gather(1)
    residual_out[...] = residual
    finish_sends(0)

    last, _ = product(1, lambda: None)
    image_out[...] = vec_a[...]
    gram_out[...] = last * (1.0 / (N_ROW * N_COL * SEGB * TILE))
    finish_sends(1)


def lay_flat(residual, image, gram, residual_out, image_out, gram_out, temp, by_row):
    for source, target in ((residual, residual_out), (image, image_out)):
        by_vector_to_by_row(source, temp, by_row)
        by_row_to_flat(by_row, target)
    gram_out[...] = gram[...]


def local(block_x, tile_values, row_block, col_block, tile_counts):
    vmem = pl.BlockSpec(memory_space=pltpu.VMEM)
    smem = pl.BlockSpec(memory_space=pltpu.SMEM)
    kinds = 7
    vectors = (
        jax.ShapeDtypeStruct((SEGB, WIDTH), F32),
        jax.ShapeDtypeStruct((SEGB, WIDTH), F32),
        jax.ShapeDtypeStruct((K, K), F32),
    )
    results = pl.pallas_call(
        kernel,
        out_shape=vectors,
        in_specs=[vmem, pl.BlockSpec(memory_space=pl.ANY), smem, smem, smem, vmem, vmem],
        out_specs=(vmem, vmem, vmem),
        scratch_shapes=[
            pltpu.VMEM((SLOTS // 64, 4, 16, TILE * TILE), BF16),
            pltpu.VMEM((16 * STAGE_PITCH, 128), F32),
            pltpu.VMEM((GROUPS, 128, 128), BF16),
            pltpu.VMEM((GROUPS, 128, 128), BF16),
            pltpu.VMEM((RB, 2, K, 128), BF16),
            pltpu.VMEM((CB, 2, K, 128), BF16),
            pltpu.VMEM((2 * RB, 512), BF16),
            pltpu.VMEM((2 * CB, 512), BF16),
            pltpu.VMEM((K * Y_PITCH, 128), F32),
            pltpu.VMEM((K * Y_PITCH, 128), F32),
            pltpu.VMEM((N_COL * 128, 128), F32),
            pltpu.VMEM((K, WIDTH), F32),
            pltpu.VMEM((K, WIDTH), F32),
            pltpu.VMEM((2, K, WIDTH), BF16),
            pltpu.VMEM((2, N_ROW, K, WIDTH), BF16),
            pltpu.VMEM((2, N_COL, K, WIDTH), BF16),
            pltpu.VMEM((2, N_ROW, K, WIDTH), BF16),
            pltpu.VMEM((2, N_COL, K, WIDTH), BF16),
            pltpu.VMEM((2, N_ROW, K, WIDTH), BF16),
            pltpu.VMEM((2, N_COL, K, WIDTH), BF16),
            pltpu.VMEM((6, K, 128), F32),
            pltpu.VMEM((3, N_ROW, K, 128), F32),
            pltpu.VMEM((3, N_COL, K, 128), F32),
            pltpu.SemaphoreType.DMA((SLOTS // 64, 4)),
            pltpu.SemaphoreType.DMA((kinds,)),
            pltpu.SemaphoreType.DMA((kinds,)),
            pltpu.SemaphoreType.DMA((4, N_ROW)),
            pltpu.SemaphoreType.DMA((4, N_COL)),
            pltpu.SemaphoreType.DMA((3,)),
            pltpu.SemaphoreType.DMA((3,)),
        ],
        compiler_params=pltpu.CompilerParams(
            collective_id=0, has_side_effects=True, vmem_limit_bytes=58 << 20
        ),
        cost_estimate=pl.CostEstimate(flops=1 << 30, bytes_accessed=9 << 20, transcendentals=0),
    )(block_x, tile_values, row_block, col_block, tile_counts, row_block, col_block)
    return pl.pallas_call(
        lay_flat,
        out_shape=vectors,
        in_specs=[vmem] * 3,
        out_specs=(vmem, vmem, vmem),
        scratch_shapes=[pltpu.VMEM((128, 128), F32), pltpu.VMEM((128, 128), F32)],
    )(*results)


def solution(mesh):
    placed = (
        P(("row", "col"), None),
        P("row", "col", None, None),
        P("row", "col", None),
        P("row", "col", None),
        P("row", "col"),
    )
    return jax.shard_map(
        local,
        mesh=mesh,
        in_specs=placed,
        out_specs=(P(("row", "col"), None), P(("row", "col"), None), P()),
        check_vma=False,
    )
```

```python
import functools

import jax
import jax.numpy as jnp
from jax import lax
from jax.experimental import pallas as pl
from jax.experimental.pallas import tpu as pltpu
from jax.sharding import PartitionSpec as P

F32 = jnp.float32
BF16 = jnp.bfloat16
TILE = 64
K = 16
SEGB = 16
SLOTS = 1024
GROUPS = SLOTS // 4
WIDTH = K * TILE
N_ROW = 8
N_COL = 16
N_CHIP = N_COL // 2
RB = N_ROW * SEGB
CB = N_COL * SEGB
STAGE_PITCH = 136
Y_PITCH = 520
EARLY_CHUNKS = 8
HIGHEST = lax.Precision.HIGHEST
NT = (((1,), (1,)), ((), ()))
NN = (((1,), (0,)), ((), ()))


def left_half(rows):
    return lax.broadcasted_iota(jnp.int32, (rows, 128), 1) < TILE


def swap_halves(value):
    return pltpu.roll(value, TILE, 1)


def lane_block(index):
    start = index * 128
    if not isinstance(index, int):
        start = pl.multiple_of(start, 128)
    return pl.ds(start, 128)


def flat_to_by_vector(flat, temp, out):
    lt = left_half(8)

    def step(pair, carry):
        low = flat[0:8, lane_block(pair)]
        high = flat[8:16, lane_block(pair)]
        temp[pl.ds(2 * pair, 8, stride=K), :] = jnp.where(lt, low, swap_halves(high))
        temp[pl.ds(2 * pair + 1, 8, stride=K), :] = jnp.where(lt, swap_halves(low), high)
        return carry

    lax.fori_loop(0, K // 2, step, 0, unroll=True)
    gather_blocks(temp, out)


def gather_blocks(temp, out):
    def step(p, carry):
        out[:, lane_block(p)] = temp[pl.ds(pl.multiple_of(p * K, K), K), :]
        return carry

    lax.fori_loop(0, 8, step, 0, unroll=True)


def by_vector_to_by_row(by_vector, temp, out):
    def spread(p, carry):
        temp[pl.ds(pl.multiple_of(p * K, K), K), :] = by_vector[:, lane_block(p)]
        return carry

    def collect(k, carry):
        out[pl.ds(pl.multiple_of(k * 8, 8), 8), :] = temp[pl.ds(k, 8, stride=K), :]
        return carry

    lax.fori_loop(0, 8, spread, 0, unroll=True)
    lax.fori_loop(0, K, collect, 0, unroll=True)


def by_row_to_flat(by_row, flat):
    lt = left_half(8)

    def step(pair, carry):
        even = by_row[pl.ds(pl.multiple_of(pair * 16, 8), 8), :]
        odd = by_row[pl.ds(pl.multiple_of(pair * 16 + 8, 8), 8), :]
        flat[0:8, lane_block(pair)] = jnp.where(lt, even, swap_halves(odd))
        flat[8:16, lane_block(pair)] = jnp.where(lt, swap_halves(even), odd)
        return carry

    lax.fori_loop(0, K // 2, step, 0, unroll=True)


def load_groups(raw, stage, tiles, chunk, count):
    lt = left_half(16)
    lane_row = lax.broadcasted_iota(jnp.int32, (16, 128), 0)

    def half(a, carry):
        live = [lane_row + ((2 * a + b) * GROUPS + chunk * 16) < count for b in range(2)]

        def step(m, inner):
            first = jnp.where(live[0], raw[chunk, 2 * a, :, lane_block(m)].astype(F32), 0.0)
            second = jnp.where(live[1], raw[chunk, 2 * a + 1, :, lane_block(m)].astype(F32), 0.0)
            even = jnp.where(lt, first, swap_halves(second))
            odd = jnp.where(lt, swap_halves(first), second)
            for h in range(2):
                base = h * 8 * STAGE_PITCH + a * TILE + 2 * m
                stage[pl.ds(base, 8, stride=STAGE_PITCH), :] = even[h * 8 : h * 8 + 8]
                stage[pl.ds(base + 1, 8, stride=STAGE_PITCH), :] = odd[h * 8 : h * 8 + 8]
            return inner

        return lax.fori_loop(0, 32, step, carry, unroll=True)

    lax.fori_loop(0, 2, half, 0, unroll=True)

    def narrow(u, carry):
        tiles[chunk * 16 + u] = stage[pl.ds(pl.multiple_of(u * STAGE_PITCH, 8), 128), :].astype(BF16)
        return carry

    lax.fori_loop(0, 16, narrow, 0, unroll=True)


def fill_table(own, table, base):
    lt = left_half(16)
    zero = jnp.zeros((16, 128), BF16)

    def step(p, carry):
        both = own[:, lane_block(p)]
        turned = swap_halves(both)
        table[base + p, 0] = jnp.where(lt, both, zero)
        table[base + p, 1] = jnp.where(lt, zero, turned)
        table[base + 8 + p, 0] = jnp.where(lt, turned, zero)
        table[base + 8 + p, 1] = jnp.where(lt, zero, both)
        return carry

    lax.fori_loop(0, 8, step, 0, unroll=True)


def multiply(index, table, tiles, products, forward, turned=None):
    lt = left_half(16)

    def step(q, carry):
        picked = [table[index[0, 0, g * GROUPS + q], (g % 2) if forward else (g // 2)] for g in range(4)]
        left = jnp.concatenate(picked, axis=0)
        matrix = tiles[q]
        if turned is not None:
            turned[q] = matrix.T
        out = lax.dot_general(left, matrix, NN, preferred_element_type=F32)
        for s in range(2):
            one, two = (s, 2 + s) if forward else (2 * s, 2 * s + 1)
            merged = jnp.where(lt, out[one * 16 : one * 16 + 16], out[two * 16 : two * 16 + 16])
            place = s * GROUPS + q
            products[pl.ds(place, 8, stride=Y_PITCH), :] = merged[:8]
            products[pl.ds(8 * Y_PITCH + place, 8, stride=Y_PITCH), :] = merged[8:]
        return carry

    lax.fori_loop(0, GROUPS, step, 0, unroll=64)


def add_up(places, products, temp, blocks):
    lt = left_half(8)
    targets = blocks // SEGB

    def step(pair, carry):
        part = [
            products[pl.ds(pl.multiple_of((2 * pair + i) * Y_PITCH, 8), SLOTS // 2), :].astype(BF16) for i in range(2)
        ]
        total = jnp.dot(places[...], jnp.concatenate(part, axis=1), preferred_element_type=F32)
        for target in range(targets):
            for i in range(2):
                half = []
                for h in range(2):
                    first = target * SEGB + h * 8
                    left = total[first : first + 8, i * 128 : i * 128 + 128]
                    right = total[blocks + first : blocks + first + 8, i * 128 : i * 128 + 128]
                    both = jnp.where(lt, left, right)
                    half.append(both + swap_halves(both))
                temp[pl.ds(target * 128 + 2 * pair + i, 8, stride=K), :] = jnp.where(lt, half[0], half[1])
        return carry

    lax.fori_loop(0, K // 2, step, 0, unroll=True)


def narrow_sums(temp, first, stride, out, count):
    def step(target, carry):
        for p in range(8):
            start = (first + target * stride) * 128 + p * K
            out[target, :, p * 128 : p * 128 + 128] = temp[pl.ds(pl.multiple_of(start, K), K), :].astype(BF16)
        return carry

    lax.fori_loop(0, count, step, 0, unroll=True)


def add_pair(temp, first, other, out, count):
    def step(target, carry):
        for p in range(8):
            start = (first + target * 2) * 128 + p * K
            here = temp[pl.ds(pl.multiple_of(start, K), K), :]
            lanes = slice(p * 128, p * 128 + 128)
            out[target, :, lanes] = (here + other[target, :, lanes].astype(F32)).astype(BF16)
        return carry

    lax.fori_loop(0, count, step, 0, unroll=True)


def factor(norm):
    row = lax.broadcasted_iota(jnp.int32, (K, K), 0)
    lane = lax.broadcasted_iota(jnp.int32, (K, K), 1)

    def step(j, carry):
        matrix, inverse = carry
        pivot_row = jnp.sum(jnp.where(row == j, matrix, 0.0), axis=0, keepdims=True)
        pivot_inv = jnp.sum(jnp.where(row == j, inverse, 0.0), axis=0, keepdims=True)
        column = jnp.sum(jnp.where(lane == j, matrix, 0.0), axis=1, keepdims=True)
        pivot = jnp.sum(jnp.where((lane == j) & (row == j), matrix, 0.0), keepdims=True)
        scale = jnp.where(row[:, 0:1] > j, column / pivot, 0.0)
        return matrix - scale * pivot_row, inverse - scale * pivot_inv

    start = (norm, jnp.where(row == lane, 1.0, 0.0).astype(F32))
    matrix, inverse = lax.fori_loop(0, K, step, start)
    diagonal = jnp.sum(jnp.where(row == lane, matrix, 0.0), axis=1, keepdims=True)
    return inverse, 1.0 / diagonal


def kernel(
    block_x, tile_values, row_s, col_s, count_s, row_v, col_v,
    residual_out, image_out, gram_out,
    raw, stage, tiles, turned, table_r, table_c, place_r, place_c, prod_r, prod_c,
    temp, vec_x, vec_a, own, got_r, got_c, part_r, part_c, pair_c, both_c, sum_r, sum_c, gram_own, gram_r, gram_c,
    load_sem, send_r, send_c, recv_r, recv_c, recv_sum_r, recv_sum_c, pair_sem, gram_recv_r, gram_recv_c,
):
    my_row, my_col = lax.axis_index("row"), lax.axis_index("col")
    my_chip, my_core = my_col // 2, lax.rem(my_col, 2)
    sibling = my_chip * 2 + 1 - my_core

    def send(axis, peer, source, target, sent, arrived):
        pltpu.make_async_remote_copy(
            src_ref=source, dst_ref=target, send_sem=sent, recv_sem=arrived,
            device_id={axis: peer}, device_id_type=pl.DeviceIdType.MESH,
        ).start()

    def others(size, me, use):
        def step(d, carry):
            use(lax.rem(me + d, size))
            return carry

        lax.fori_loop(1, size, step, 0)

    def wait_bytes(block, sem):
        pltpu.make_async_copy(block, block, sem).wait()

    def load(chunk, g):
        return pltpu.make_async_copy(
            tile_values.at[0, 0, pl.ds(pl.multiple_of(g * GROUPS + chunk * 16, 16), 16), :],
            raw.at[chunk, g], load_sem.at[chunk, g],
        )

    def start_load(chunk, carry):
        for g in range(4):
            load(chunk, g).start()
        return carry

    barrier = pltpu.get_barrier_semaphore()

    def greet(axis, peer):
        pl.semaphore_signal(barrier, inc=1, device_id={axis: peer}, device_id_type=pl.DeviceIdType.MESH)

    others(N_ROW, my_row, lambda peer: greet("row", peer))
    others(N_COL, my_col, lambda peer: greet("col", peer))

    def put_gram(which, value):
        gram_own[which] = jnp.zeros((8, 128), F32)
        gram_own[which, :, 0:K] = value[0:8]
        gram_own[which, :, K : 2 * K] = value[8:16]

    lax.fori_loop(0, SLOTS // 64, start_load, 0)
    flat_to_by_vector(block_x, temp, vec_x)
    own[0] = vec_x[...].astype(BF16)
    norm = lax.dot_general(vec_x[...], vec_x[...], NT, precision=HIGHEST, preferred_element_type=F32)
    put_gram(0, norm)
    count = count_s[0, 0]

    def arrange(chunk, carry):
        for g in range(4):
            load(chunk, g).wait()
        load_groups(raw, stage, tiles, chunk, count)
        return carry

    lax.fori_loop(0, EARLY_CHUNKS, arrange, 0)
    pl.semaphore_wait(barrier, N_ROW + N_COL - 2)

    def gather(step):
        def to_row(peer):
            send("row", peer, own.at[step], got_r.at[step, my_row], send_r.at[step], recv_r.at[step, my_row])

        def to_col(peer):
            send("col", peer, own.at[step], got_c.at[step, my_col], send_c.at[step], recv_c.at[step, my_col])

        others(N_ROW, my_row, to_row)
        others(N_CHIP, my_chip, lambda chip: to_col(chip * 2 + my_core))
        to_col(sibling)
        got_c[step, my_col] = own[step]

    def forward(step):
        def pass_on(chip):
            slot = chip * 2 + my_core
            wait_bytes(got_c.at[step, slot], recv_c.at[step, slot])
            send(
                "col", sibling, got_c.at[step, slot], got_c.at[step, slot], send_c.at[step], recv_c.at[step, slot]
            )

        others(N_CHIP, my_chip, pass_on)

    def gram_row(which):
        def to_row(peer):
            send(
                "row", peer, gram_own.at[which], gram_r.at[which, my_row], send_r.at[4 + which], gram_recv_r.at[which]
            )

        others(N_ROW, my_row, to_row)
        gram_r[which, my_row] = gram_own[which]

    def gram_col(which):
        wait_bytes(gram_r.at[which, pl.ds(0, N_ROW - 1)], gram_recv_r.at[which])
        gram_own[3 + which] = jnp.sum(gram_r[which], axis=0)

        def to_col(peer):
            send(
                "col", peer, gram_own.at[3 + which], gram_c.at[which, my_col], send_c.at[4 + which],
                gram_recv_c.at[which],
            )

        others(N_COL, my_col, to_col)
        gram_c[which, my_col] = gram_own[3 + which]

    def gram_done(which):
        wait_bytes(gram_c.at[which, pl.ds(0, N_COL - 1)], gram_recv_c.at[which])
        total = jnp.sum(gram_c[which], axis=0)
        return jnp.concatenate([total[:, 0:K], total[:, K : 2 * K]], axis=0)

    def cross_part(step):
        def dot(chip, carry):
            slot = chip * 2 + my_core
            return carry + lax.dot_general(both_c[step, chip], got_c[step, slot], NT, preferred_element_type=F32)

        return lax.fori_loop(0, N_CHIP, dot, jnp.zeros((K, K), F32), unroll=True)

    def finish_sends(step):
        wait_bytes(got_r.at[step, pl.ds(0, N_ROW - 1)], send_r.at[step])
        wait_bytes(got_c.at[step, pl.ds(0, N_COL - 1)], send_c.at[step])
        wait_bytes(got_r.at[step, pl.ds(0, N_ROW - 1)], send_r.at[2 + step])
        wait_bytes(got_c.at[step, pl.ds(0, N_COL - 1)], send_c.at[2 + step])
        for which in (0, 1) if step == 0 else (2,):
            wait_bytes(gram_r.at[which, pl.ds(0, N_ROW - 1)], send_r.at[4 + which])
            wait_bytes(gram_c.at[which, pl.ds(0, N_COL - 1)], send_c.at[4 + which])

    gather(0)
    gram_row(0)
    lax.fori_loop(EARLY_CHUNKS, SLOTS // 64, arrange, 0)
    for s in range(2):
        columns = jnp.concatenate(
            [col_v[0, :, s * 256 : s * 256 + 256], col_v[0, :, 512 + s * 256 : 768 + s * 256]], axis=1
        )
        hit = lax.broadcasted_iota(jnp.int32, (CB, 512), 0) == columns
        place_c[s * CB : s * CB + CB, :] = jnp.where(hit, 1.0, 0.0).astype(BF16)
        hit = lax.broadcasted_iota(jnp.int32, (RB, 512), 0) == row_v[0, :, s * 512 : s * 512 + 512]
        place_r[s * RB : s * RB + RB, :] = jnp.where(hit, 1.0, 0.0).astype(BF16)
    gram_col(0)

    def product(step, while_waiting):
        def enter_row(peer):
            wait_bytes(got_r.at[step, peer], recv_r.at[step, peer])
            fill_table(got_r.at[step, peer], table_r, peer * SEGB)

        def enter_same(chip):
            slot = chip * 2 + my_core
            fill_table(got_c.at[step, slot], table_c, slot * SEGB)

        def enter_other(chip):
            slot = chip * 2 + 1 - my_core
            wait_bytes(got_c.at[step, slot], recv_c.at[step, slot])
            fill_table(got_c.at[step, slot], table_c, slot * SEGB)

        fill_table(own.at[step], table_r, my_row * SEGB)
        others(N_ROW, my_row, enter_row)
        multiply(row_s, table_r, tiles, prod_c, False, turned if step == 0 else None)
        forward(step)
        add_up(place_c, prod_c, temp, CB)
        narrow_sums(temp, 1 - my_core, 2, part_c.at[step], N_CHIP)
        send("col", sibling, part_c.at[step], pair_c.at[step], send_c.at[2 + step], pair_sem.at[step])
        enter_same(my_chip)
        others(N_CHIP, my_chip, enter_same)
        enter_other(my_chip)
        others(N_CHIP, my_chip, enter_other)
        wait_bytes(pair_c.at[step], pair_sem.at[step])
        add_pair(temp, my_core, pair_c.at[step], both_c.at[step], N_CHIP)
        put_gram(1 + step, cross_part(step))
        gram_row(1 + step)

        def sums_to_col(chip):
            send(
                "col", chip * 2 + my_core, both_c.at[step, chip], sum_c.at[step, my_chip], send_c.at[2 + step],
                recv_sum_c.at[step, my_chip],
            )

        others(N_CHIP, my_chip, sums_to_col)
        multiply(col_s, table_c, turned, prod_r, True)
        add_up(place_r, prod_r, temp, RB)
        narrow_sums(temp, 0, 1, part_r.at[step], N_ROW)
        gram_col(1 + step)

        def sums_to_row(peer):
            send(
                "row", peer, part_r.at[step, peer], sum_r.at[step, my_row], send_r.at[2 + step],
                recv_sum_r.at[step, my_row],
            )

        others(N_ROW, my_row, sums_to_row)
        extra = while_waiting()
        vec_a[...] = both_c[step, my_chip].astype(F32) + part_r[step, my_row].astype(F32)

        def add_col(chip):
            wait_bytes(sum_c.at[step, chip], recv_sum_c.at[step, chip])
            vec_a[...] += sum_c[step, chip].astype(F32)

        def add_row(peer):
            wait_bytes(sum_r.at[step, peer], recv_sum_r.at[step, peer])
            vec_a[...] += sum_r[step, peer].astype(F32)

        others(N_CHIP, my_chip, add_col)
        others(N_ROW, my_row, add_row)
        half = gram_done(1 + step)
        return half + half.T, extra

    cross, (inverse, scale) = product(0, lambda: factor(gram_done(0)))
    halfway = lax.dot_general(inverse, cross, NT, precision=HIGHEST, preferred_element_type=F32) * scale
    coupling = lax.dot_general(
        halfway, inverse, (((0,), (0,)), ((), ())), precision=HIGHEST, preferred_element_type=F32
    )
    residual = vec_a[...] - jnp.dot(coupling, vec_x[...], precision=HIGHEST, preferred_element_type=F32)
    own[1] = residual.astype(BF16)
    gather(1)
    residual_out[...] = residual
    finish_sends(0)

    last, _ = product(1, lambda: None)
    image_out[...] = vec_a[...]
    gram_out[...] = last * (1.0 / (N_ROW * N_COL * SEGB * TILE))
    finish_sends(1)


def lay_flat(residual, image, gram, residual_out, image_out, gram_out, temp, by_row):
    for source, target in ((residual, residual_out), (image, image_out)):
        by_vector_to_by_row(source, temp, by_row)
        by_row_to_flat(by_row, target)
    gram_out[...] = gram[...]


def local(block_x, tile_values, row_block, col_block, tile_counts):
    vmem = pl.BlockSpec(memory_space=pltpu.VMEM)
    smem = pl.BlockSpec(memory_space=pltpu.SMEM)
    kinds = 7
    vectors = (
        jax.ShapeDtypeStruct((SEGB, WIDTH), F32),
        jax.ShapeDtypeStruct((SEGB, WIDTH), F32),
        jax.ShapeDtypeStruct((K, K), F32),
    )
    results = pl.pallas_call(
        kernel,
        out_shape=vectors,
        in_specs=[vmem, pl.BlockSpec(memory_space=pl.ANY), smem, smem, smem, vmem, vmem],
        out_specs=(vmem, vmem, vmem),
        scratch_shapes=[
            pltpu.VMEM((SLOTS // 64, 4, 16, TILE * TILE), BF16),
            pltpu.VMEM((16 * STAGE_PITCH, 128), F32),
            pltpu.VMEM((GROUPS, 128, 128), BF16),
            pltpu.VMEM((GROUPS, 128, 128), BF16),
            pltpu.VMEM((RB, 2, K, 128), BF16),
            pltpu.VMEM((CB, 2, K, 128), BF16),
            pltpu.VMEM((2 * RB, 512), BF16),
            pltpu.VMEM((2 * CB, 512), BF16),
            pltpu.VMEM((K * Y_PITCH, 128), F32),
            pltpu.VMEM((K * Y_PITCH, 128), F32),
            pltpu.VMEM((N_COL * 128, 128), F32),
            pltpu.VMEM((K, WIDTH), F32),
            pltpu.VMEM((K, WIDTH), F32),
            pltpu.VMEM((2, K, WIDTH), BF16),
            pltpu.VMEM((2, N_ROW, K, WIDTH), BF16),
            pltpu.VMEM((2, N_COL, K, WIDTH), BF16),
            pltpu.VMEM((2, N_ROW, K, WIDTH), BF16),
            pltpu.VMEM((2, N_CHIP, K, WIDTH), BF16),
            pltpu.VMEM((2, N_CHIP, K, WIDTH), BF16),
            pltpu.VMEM((2, N_CHIP, K, WIDTH), BF16),
            pltpu.VMEM((2, N_ROW, K, WIDTH), BF16),
            pltpu.VMEM((2, N_CHIP, K, WIDTH), BF16),
            pltpu.VMEM((6, 8, 128), F32),
            pltpu.VMEM((3, N_ROW, 8, 128), F32),
            pltpu.VMEM((3, N_COL, 8, 128), F32),
            pltpu.SemaphoreType.DMA((SLOTS // 64, 4)),
            pltpu.SemaphoreType.DMA((kinds,)),
            pltpu.SemaphoreType.DMA((kinds,)),
            pltpu.SemaphoreType.DMA((2, N_ROW)),
            pltpu.SemaphoreType.DMA((2, N_COL)),
            pltpu.SemaphoreType.DMA((2, N_ROW)),
            pltpu.SemaphoreType.DMA((2, N_CHIP)),
            pltpu.SemaphoreType.DMA((2,)),
            pltpu.SemaphoreType.DMA((3,)),
            pltpu.SemaphoreType.DMA((3,)),
        ],
        compiler_params=pltpu.CompilerParams(
            collective_id=0, has_side_effects=True, vmem_limit_bytes=58 << 20
        ),
        cost_estimate=pl.CostEstimate(flops=1 << 30, bytes_accessed=9 << 20, transcendentals=0),
    )(block_x, tile_values, row_block, col_block, tile_counts, row_block, col_block)
    return pl.pallas_call(
        lay_flat,
        out_shape=vectors,
        in_specs=[vmem] * 3,
        out_specs=(vmem, vmem, vmem),
        scratch_shapes=[pltpu.VMEM((128, 128), F32), pltpu.VMEM((128, 128), F32)],
    )(*results)


def solution(mesh):
    placed = (
        P(("row", "col"), None),
        P("row", "col", None, None),
        P("row", "col", None),
        P("row", "col", None),
        P("row", "col"),
    )
    return jax.shard_map(
        local,
        mesh=mesh,
        in_specs=placed,
        out_specs=(P(("row", "col"), None), P(("row", "col"), None), P()),
        check_vma=False,
    )
```

```python
import functools

import jax
import jax.numpy as jnp
from jax import lax
from jax.experimental import pallas as pl
from jax.experimental.pallas import tpu as pltpu
from jax.sharding import PartitionSpec as P

F32 = jnp.float32
BF16 = jnp.bfloat16
TILE = 64
K = 16
SEGB = 16
SLOTS = 1024
GROUPS = SLOTS // 4
WIDTH = K * TILE
N_ROW = 8
N_COL = 16
N_CHIP = N_COL // 2
RB = N_ROW * SEGB
CB = N_COL * SEGB
STAGE_PITCH = 136
Y_PITCH = 520
EARLY_CHUNKS = 8
HIGHEST = lax.Precision.HIGHEST
NT = (((1,), (1,)), ((), ()))
NN = (((1,), (0,)), ((), ()))


def left_half(rows):
    return lax.broadcasted_iota(jnp.int32, (rows, 128), 1) < TILE


def swap_halves(value):
    return pltpu.roll(value, TILE, 1)


def lane_block(index):
    start = index * 128
    if not isinstance(index, int):
        start = pl.multiple_of(start, 128)
    return pl.ds(start, 128)


def flat_to_by_vector(flat, temp, out):
    lt = left_half(8)

    def step(pair, carry):
        low = flat[0:8, lane_block(pair)]
        high = flat[8:16, lane_block(pair)]
        temp[pl.ds(2 * pair, 8, stride=K), :] = jnp.where(lt, low, swap_halves(high))
        temp[pl.ds(2 * pair + 1, 8, stride=K), :] = jnp.where(lt, swap_halves(low), high)
        return carry

    lax.fori_loop(0, K // 2, step, 0, unroll=True)
    gather_blocks(temp, out)


def gather_blocks(temp, out):
    def step(p, carry):
        out[:, lane_block(p)] = temp[pl.ds(pl.multiple_of(p * K, K), K), :]
        return carry

    lax.fori_loop(0, 8, step, 0, unroll=True)


def by_vector_to_by_row(by_vector, temp, out):
    def spread(p, carry):
        temp[pl.ds(pl.multiple_of(p * K, K), K), :] = by_vector[:, lane_block(p)]
        return carry

    def collect(k, carry):
        out[pl.ds(pl.multiple_of(k * 8, 8), 8), :] = temp[pl.ds(k, 8, stride=K), :]
        return carry

    lax.fori_loop(0, 8, spread, 0, unroll=True)
    lax.fori_loop(0, K, collect, 0, unroll=True)


def by_row_to_flat(by_row, flat):
    lt = left_half(8)

    def step(pair, carry):
        even = by_row[pl.ds(pl.multiple_of(pair * 16, 8), 8), :]
        odd = by_row[pl.ds(pl.multiple_of(pair * 16 + 8, 8), 8), :]
        flat[0:8, lane_block(pair)] = jnp.where(lt, even, swap_halves(odd))
        flat[8:16, lane_block(pair)] = jnp.where(lt, swap_halves(even), odd)
        return carry

    lax.fori_loop(0, K // 2, step, 0, unroll=True)


def load_groups(raw, stage, tiles, chunk, count):
    lt = left_half(16)
    lane_row = lax.broadcasted_iota(jnp.int32, (16, 128), 0)

    def half(a, carry):
        live = [lane_row + ((2 * a + b) * GROUPS + chunk * 16) < count for b in range(2)]

        def step(m, inner):
            first = jnp.where(live[0], raw[chunk, 2 * a, :, lane_block(m)].astype(F32), 0.0)
            second = jnp.where(live[1], raw[chunk, 2 * a + 1, :, lane_block(m)].astype(F32), 0.0)
            even = jnp.where(lt, first, swap_halves(second))
            odd = jnp.where(lt, swap_halves(first), second)
            for h in range(2):
                base = h * 8 * STAGE_PITCH + a * TILE + 2 * m
                stage[pl.ds(base, 8, stride=STAGE_PITCH), :] = even[h * 8 : h * 8 + 8]
                stage[pl.ds(base + 1, 8, stride=STAGE_PITCH), :] = odd[h * 8 : h * 8 + 8]
            return inner

        return lax.fori_loop(0, 32, step, carry, unroll=True)

    lax.fori_loop(0, 2, half, 0, unroll=True)

    def narrow(u, carry):
        tiles[chunk * 16 + u] = stage[pl.ds(pl.multiple_of(u * STAGE_PITCH, 8), 128), :].astype(BF16)
        return carry

    lax.fori_loop(0, 16, narrow, 0, unroll=True)


def fill_table(own, table, base):
    lt = left_half(16)
    zero = jnp.zeros((16, 128), BF16)

    def step(p, carry):
        both = own[:, lane_block(p)]
        turned = swap_halves(both)
        table[base + p, 0] = jnp.where(lt, both, zero)
        table[base + p, 1] = jnp.where(lt, zero, turned)
        table[base + 8 + p, 0] = jnp.where(lt, turned, zero)
        table[base + 8 + p, 1] = jnp.where(lt, zero, both)
        return carry

    lax.fori_loop(0, 8, step, 0, unroll=True)


def multiply(index, table, tiles, products, forward, turned=None):
    lt = left_half(16)

    def step(q, carry):
        picked = [table[index[0, 0, g * GROUPS + q], (g % 2) if forward else (g // 2)] for g in range(4)]
        left = jnp.concatenate(picked, axis=0)
        matrix = tiles[q]
        if turned is not None:
            turned[q] = matrix.T
        out = lax.dot_general(left, matrix, NN, preferred_element_type=F32)
        for s in range(2):
            one, two = (s, 2 + s) if forward else (2 * s, 2 * s + 1)
            merged = jnp.where(lt, out[one * 16 : one * 16 + 16], out[two * 16 : two * 16 + 16])
            place = s * GROUPS + q
            products[pl.ds(place, 8, stride=Y_PITCH), :] = merged[:8]
            products[pl.ds(8 * Y_PITCH + place, 8, stride=Y_PITCH), :] = merged[8:]
        return carry

    lax.fori_loop(0, GROUPS, step, 0, unroll=128)


def add_up(places, products, temp, blocks):
    lt = left_half(8)
    targets = blocks // SEGB

    def step(pair, carry):
        part = [
            products[pl.ds(pl.multiple_of((2 * pair + i) * Y_PITCH, 8), SLOTS // 2), :].astype(BF16) for i in range(2)
        ]
        total = jnp.dot(places[...], jnp.concatenate(part, axis=1), preferred_element_type=F32)
        for target in range(targets):
            for i in range(2):
                half = []
                for h in range(2):
                    first = target * SEGB + h * 8
                    left = total[first : first + 8, i * 128 : i * 128 + 128]
                    right = total[blocks + first : blocks + first + 8, i * 128 : i * 128 + 128]
                    both = jnp.where(lt, left, right)
                    half.append(both + swap_halves(both))
                temp[pl.ds(target * 128 + 2 * pair + i, 8, stride=K), :] = jnp.where(lt, half[0], half[1])
        return carry

    lax.fori_loop(0, K // 2, step, 0, unroll=True)


def narrow_sums(temp, first, stride, out, count):
    def step(target, carry):
        for p in range(8):
            start = (first + target * stride) * 128 + p * K
            out[target, :, p * 128 : p * 128 + 128] = temp[pl.ds(pl.multiple_of(start, K), K), :].astype(BF16)
        return carry

    lax.fori_loop(0, count, step, 0, unroll=True)


def add_pair(temp, first, other, out, count):
    def step(target, carry):
        for p in range(8):
            start = (first + target * 2) * 128 + p * K
            here = temp[pl.ds(pl.multiple_of(start, K), K), :]
            lanes = slice(p * 128, p * 128 + 128)
            out[target, :, lanes] = (here + other[target, :, lanes].astype(F32)).astype(BF16)
        return carry

    lax.fori_loop(0, count, step, 0, unroll=True)


def factor(norm):
    row = lax.broadcasted_iota(jnp.int32, (K, K), 0)
    lane = lax.broadcasted_iota(jnp.int32, (K, K), 1)

    def step(j, carry):
        matrix, inverse = carry
        pivot_row = jnp.sum(jnp.where(row == j, matrix, 0.0), axis=0, keepdims=True)
        pivot_inv = jnp.sum(jnp.where(row == j, inverse, 0.0), axis=0, keepdims=True)
        column = jnp.sum(jnp.where(lane == j, matrix, 0.0), axis=1, keepdims=True)
        pivot = jnp.sum(jnp.where((lane == j) & (row == j), matrix, 0.0), keepdims=True)
        scale = jnp.where(row[:, 0:1] > j, column / pivot, 0.0)
        return matrix - scale * pivot_row, inverse - scale * pivot_inv

    start = (norm, jnp.where(row == lane, 1.0, 0.0).astype(F32))
    matrix, inverse = lax.fori_loop(0, K, step, start)
    diagonal = jnp.sum(jnp.where(row == lane, matrix, 0.0), axis=1, keepdims=True)
    return inverse, 1.0 / diagonal


def kernel(
    block_x, tile_values, row_block, col_block, tile_counts,
    residual_out, image_out, gram_out,
    raw, stage, tiles, turned, table_r, table_c, place_r, place_c, prod_r, prod_c,
    flat_x, row_s, col_s, count_s, row_v, col_v, temp, by_row, vec_x, vec_a, vec_b, gram_last, own, got_r, got_c, part_r, part_c, pair_c, both_c, spare, sum_r, sum_c, gram_own, gram_r, gram_c,
    enter_sem, leave_sem, load_sem, send_r, send_c, recv_r, recv_c, recv_sum_r, recv_sum_c, pair_sem, gram_recv_r, gram_recv_c,
):
    my_row, my_col = lax.axis_index("row"), lax.axis_index("col")
    my_chip, my_core = my_col // 2, lax.rem(my_col, 2)
    sibling = my_chip * 2 + 1 - my_core

    def send(axis, peer, source, target, sent, arrived):
        pltpu.make_async_remote_copy(
            src_ref=source, dst_ref=target, send_sem=sent, recv_sem=arrived,
            device_id={axis: peer}, device_id_type=pl.DeviceIdType.MESH,
        ).start()

    def others(size, me, use):
        def step(d, carry):
            use(lax.rem(me + d, size))
            return carry

        lax.fori_loop(1, size, step, 0)

    def wait_bytes(block, sem):
        pltpu.make_async_copy(block, block, sem).wait()

    def load(chunk, g):
        return pltpu.make_async_copy(
            tile_values.at[0, 0, pl.ds(pl.multiple_of(g * GROUPS + chunk * 16, 16), 16), :],
            raw.at[chunk, g], load_sem.at[chunk, g],
        )

    def start_load(chunk, carry):
        for g in range(4):
            load(chunk, g).start()
        return carry

    barrier = pltpu.get_barrier_semaphore()

    def greet(axis, peer):
        pl.semaphore_signal(barrier, inc=1, device_id={axis: peer}, device_id_type=pl.DeviceIdType.MESH)

    others(N_ROW, my_row, lambda peer: greet("row", peer))
    others(N_COL, my_col, lambda peer: greet("col", peer))

    def put_gram(which, value):
        gram_own[which] = jnp.zeros((8, 128), F32)
        gram_own[which, :, 0:K] = value[0:8]
        gram_own[which, :, K : 2 * K] = value[8:16]

    pairs = (
        (block_x, flat_x), (tile_counts, count_s), (row_block, row_s), (col_block, col_s),
        (row_block, row_v), (col_block, col_v),
    )
    enter = [pltpu.make_async_copy(a, b, enter_sem.at[i]) for i, (a, b) in enumerate(pairs)]

    def leave(which, source, target):
        return pltpu.make_async_copy(source, target, leave_sem.at[which])

    for arrival in enter:
        arrival.start()
    lax.fori_loop(0, SLOTS // 64, start_load, 0)
    enter[0].wait()
    flat_to_by_vector(flat_x, temp, vec_x)
    own[0] = vec_x[...].astype(BF16)
    norm = lax.dot_general(vec_x[...], vec_x[...], NT, precision=HIGHEST, preferred_element_type=F32)
    put_gram(0, norm)
    enter[1].wait()
    count = count_s[0, 0]

    def arrange(chunk, carry):
        for g in range(4):
            load(chunk, g).wait()
        load_groups(raw, stage, tiles, chunk, count)
        return carry

    lax.fori_loop(0, EARLY_CHUNKS, arrange, 0)
    pl.semaphore_wait(barrier, N_ROW + N_COL - 2)

    def gather(step, beside):
        def to_row(peer):
            send("row", peer, own.at[step], got_r.at[step, my_row], send_r.at[step], recv_r.at[step, my_row])

        def to_col(peer):
            send(
                "col", peer, own.at[step], got_c.at[step, my_chip, my_core], send_c.at[step], recv_c.at[step, my_col]
            )

        others(N_ROW, my_row, to_row)
        others(N_CHIP, my_chip, lambda chip: to_col(chip * 2 + my_core))
        to_col(sibling)
        got_c[step, my_chip, my_core] = own[step]
        beside()

    def forward(step):
        def pass_on(chip):
            slot = chip * 2 + my_core
            block = got_c.at[step, chip, my_core]
            wait_bytes(block, recv_c.at[step, slot])
            send("col", sibling, block, block, send_c.at[step], recv_c.at[step, slot])

        others(N_CHIP, my_chip, pass_on)

    def gram_row(which):
        def to_row(peer):
            send(
                "row", peer, gram_own.at[which], gram_r.at[which, my_row], send_r.at[4 + which], gram_recv_r.at[which]
            )

        others(N_ROW, my_row, to_row)
        gram_r[which, my_row] = gram_own[which]

    def gram_col(which):
        wait_bytes(gram_r.at[which, pl.ds(0, N_ROW - 1)], gram_recv_r.at[which])
        gram_own[3 + which] = jnp.sum(gram_r[which], axis=0)

        def to_col(peer):
            send(
                "col", peer, gram_own.at[3 + which], gram_c.at[which, my_col], send_c.at[4 + which],
                gram_recv_c.at[which],
            )

        others(N_COL, my_col, to_col)
        gram_c[which, my_col] = gram_own[3 + which]

    def gram_done(which):
        wait_bytes(gram_c.at[which, pl.ds(0, N_COL - 1)], gram_recv_c.at[which])
        total = jnp.sum(gram_c[which], axis=0)
        return jnp.concatenate([total[:, 0:K], total[:, K : 2 * K]], axis=0)

    def cross_part(step):
        total = jnp.zeros((K, K), F32)
        for side in range(2):
            core = my_core if side == 0 else 1 - my_core
            sums = part_c[step, side].reshape(N_CHIP * K, WIDTH)
            vectors = got_c[step, :, core].reshape(N_CHIP * K, WIDTH)
            pairs = lax.dot_general(sums, vectors, NT, preferred_element_type=F32)
            for chip in range(N_CHIP):
                total += pairs[chip * K : chip * K + K, chip * K : chip * K + K]
        return total

    def fill_all(step):
        def enter(chip, carry):
            for core in range(2):
                fill_table(got_c.at[step, chip, core], table_c, (chip * 2 + core) * SEGB)
            return carry

        lax.fori_loop(0, N_CHIP, enter, 0, unroll=4)

    def finish_sends(step):
        sent_c = spare.at[pl.ds(0, N_COL - 1)]
        wait_bytes(got_r.at[step, pl.ds(0, N_ROW - 1)], send_r.at[step])
        wait_bytes(sent_c, send_c.at[step])
        wait_bytes(got_r.at[step, pl.ds(0, N_ROW - 1)], send_r.at[2 + step])
        wait_bytes(sent_c, send_c.at[2 + step])
        for which in (0, 1) if step == 0 else (2,):
            wait_bytes(gram_r.at[which, pl.ds(0, N_ROW - 1)], send_r.at[4 + which])
            wait_bytes(gram_c.at[which, pl.ds(0, N_COL - 1)], send_c.at[4 + which])

    def arrange_rest():
        gram_row(0)
        lax.fori_loop(EARLY_CHUNKS, SLOTS // 64, arrange, 0)

    gather(0, arrange_rest)
    for arrival in enter[2:]:
        arrival.wait()
    for s in range(2):
        columns = jnp.concatenate(
            [col_v[0, :, s * 256 : s * 256 + 256], col_v[0, :, 512 + s * 256 : 768 + s * 256]], axis=1
        )
        hit = lax.broadcasted_iota(jnp.int32, (CB, 512), 0) == columns
        place_c[s * CB : s * CB + CB, :] = jnp.where(hit, 1.0, 0.0).astype(BF16)
        hit = lax.broadcasted_iota(jnp.int32, (RB, 512), 0) == row_v[0, :, s * 512 : s * 512 + 512]
        place_r[s * RB : s * RB + RB, :] = jnp.where(hit, 1.0, 0.0).astype(BF16)
    gram_col(0)

    def product(step):
        def arrive_row(peer):
            wait_bytes(got_r.at[step, peer], recv_r.at[step, peer])

        def enter_row(d, carry):
            peer = lax.rem(my_row + d, N_ROW)
            fill_table(got_r.at[step, peer], table_r, peer * SEGB)
            return carry

        def arrive_other(chip):
            wait_bytes(got_c.at[step, chip, 1 - my_core], recv_c.at[step, chip * 2 + 1 - my_core])

        fill_table(own.at[step], table_r, my_row * SEGB)
        others(N_ROW, my_row, arrive_row)
        lax.fori_loop(1, N_ROW, enter_row, 0, unroll=True)
        multiply(row_s, table_r, tiles, prod_c, False, turned if step == 0 else None)
        forward(step)
        add_up(place_c, prod_c, temp, CB)
        narrow_sums(temp, 1 - my_core, 2, part_c.at[step, 1], N_CHIP)
        send("col", sibling, part_c.at[step, 1], pair_c.at[step], send_c.at[2 + step], pair_sem.at[step])
        narrow_sums(temp, my_core, 2, part_c.at[step, 0], N_CHIP)
        arrive_other(my_chip)
        others(N_CHIP, my_chip, arrive_other)
        put_gram(1 + step, cross_part(step))
        gram_row(1 + step)
        wait_bytes(pair_c.at[step], pair_sem.at[step])
        add_pair(temp, my_core, pair_c.at[step], both_c.at[step], N_CHIP)

        def sums_to_col(chip):
            send(
                "col", chip * 2 + my_core, both_c.at[step, chip], sum_c.at[step, my_chip], send_c.at[2 + step],
                recv_sum_c.at[step, my_chip],
            )

        others(N_CHIP, my_chip, sums_to_col)
        fill_all(step)
        multiply(col_s, table_c, turned, prod_r, True)
        add_up(place_r, prod_r, temp, RB)
        narrow_sums(temp, 0, 1, part_r.at[step], N_ROW)
        gram_col(1 + step)

        def sums_to_row(peer):
            send(
                "row", peer, part_r.at[step, peer], sum_r.at[step, my_row], send_r.at[2 + step],
                recv_sum_r.at[step, my_row],
            )

        others(N_ROW, my_row, sums_to_row)
        if step == 0:
            inverse, scale = factor(gram_done(0))
            norm_inverse = lax.dot_general(
                inverse * scale, inverse, (((0,), (0,)), ((), ())), precision=HIGHEST, preferred_element_type=F32
            )

        def add_col(chip):
            wait_bytes(sum_c.at[step, chip], recv_sum_c.at[step, chip])
            vec_a[...] += sum_c[step, chip].astype(F32)

        vec_a[...] = both_c[step, my_chip].astype(F32) + part_r[step, my_row].astype(F32)
        others(N_CHIP, my_chip, add_col)
        half = gram_done(1 + step)
        cross = half + half.T
        if step == 0:
            coupling = jnp.dot(cross, norm_inverse, precision=HIGHEST, preferred_element_type=F32)
            vec_a[...] -= jnp.dot(coupling, vec_x[...], precision=HIGHEST, preferred_element_type=F32)

        def arrive_sum(peer):
            wait_bytes(sum_r.at[step, peer], recv_sum_r.at[step, peer])

        others(N_ROW, my_row, arrive_sum)
        sum_r[step, my_row] = jnp.zeros((K, WIDTH), BF16)

        def add_row(p, carry):
            total = vec_a[:, lane_block(p)]
            for slot in range(N_ROW):
                total += sum_r[step, slot, :, lane_block(p)].astype(F32)
            vec_a[:, lane_block(p)] = total
            if step == 0:
                own[1, :, lane_block(p)] = total.astype(BF16)
            return carry

        lax.fori_loop(0, 8, add_row, 0, unroll=True)
        return cross

    product(0)

    def keep_residual():
        by_vector_to_by_row(vec_a, temp, by_row)
        by_row_to_flat(by_row, vec_x)
        leave(0, vec_x, residual_out).start()
        finish_sends(0)

    gather(1, keep_residual)
    last = product(1)
    by_vector_to_by_row(vec_a, temp, by_row)
    by_row_to_flat(by_row, vec_b)
    gram_last[...] = last * (1.0 / (N_ROW * N_COL * SEGB * TILE))
    leave(1, vec_b, image_out).start()
    leave(2, gram_last, gram_out).start()
    finish_sends(1)
    leave(0, vec_x, residual_out).wait()
    leave(1, vec_b, image_out).wait()
    leave(2, gram_last, gram_out).wait()


def pass_results(residual, image, gram, residual_out, image_out, gram_out):
    residual_out[...] = residual[...]
    image_out[...] = image[...]
    gram_out[...] = gram[...]


def local(block_x, tile_values, row_block, col_block, tile_counts):
    vmem = pl.BlockSpec(memory_space=pltpu.VMEM)
    anywhere = pl.BlockSpec(memory_space=pl.ANY)
    kinds = 7
    vectors = (
        jax.ShapeDtypeStruct((SEGB, WIDTH), F32),
        jax.ShapeDtypeStruct((SEGB, WIDTH), F32),
        jax.ShapeDtypeStruct((K, K), F32),
    )
    results = pl.pallas_call(
        kernel,
        out_shape=vectors,
        in_specs=[anywhere] * 5,
        out_specs=(anywhere,) * 3,
        scratch_shapes=[
            pltpu.VMEM((SLOTS // 64, 4, 16, TILE * TILE), BF16),
            pltpu.VMEM((16 * STAGE_PITCH, 128), F32),
            pltpu.VMEM((GROUPS, 128, 128), BF16),
            pltpu.VMEM((GROUPS, 128, 128), BF16),
            pltpu.VMEM((RB, 2, K, 128), BF16),
            pltpu.VMEM((CB, 2, K, 128), BF16),
            pltpu.VMEM((2 * RB, 512), BF16),
            pltpu.VMEM((2 * CB, 512), BF16),
            pltpu.VMEM((K * Y_PITCH, 128), F32),
            pltpu.VMEM((K * Y_PITCH, 128), F32),
            pltpu.VMEM((SEGB, WIDTH), F32),
            pltpu.SMEM((1, 1, SLOTS), jnp.int32),
            pltpu.SMEM((1, 1, SLOTS), jnp.int32),
            pltpu.SMEM((1, 1), jnp.int32),
            pltpu.VMEM((1, 1, SLOTS), jnp.int32),
            pltpu.VMEM((1, 1, SLOTS), jnp.int32),
            pltpu.VMEM((N_COL * 128, 128), F32),
            pltpu.VMEM((128, 128), F32),
            pltpu.VMEM((K, WIDTH), F32),
            pltpu.VMEM((K, WIDTH), F32),
            pltpu.VMEM((K, WIDTH), F32),
            pltpu.VMEM((K, K), F32),
            pltpu.VMEM((2, K, WIDTH), BF16),
            pltpu.VMEM((2, N_ROW, K, WIDTH), BF16),
            pltpu.VMEM((2, N_CHIP, 2, K, WIDTH), BF16),
            pltpu.VMEM((2, N_ROW, K, WIDTH), BF16),
            pltpu.VMEM((2, 2, N_CHIP, K, WIDTH), BF16),
            pltpu.VMEM((2, N_CHIP, K, WIDTH), BF16),
            pltpu.VMEM((2, N_CHIP, K, WIDTH), BF16),
            pltpu.VMEM((N_COL, K, WIDTH), BF16),
            pltpu.VMEM((2, N_ROW, K, WIDTH), BF16),
            pltpu.VMEM((2, N_CHIP, K, WIDTH), BF16),
            pltpu.VMEM((6, 8, 128), F32),
            pltpu.VMEM((3, N_ROW, 8, 128), F32),
            pltpu.VMEM((3, N_COL, 8, 128), F32),
            pltpu.SemaphoreType.DMA((6,)),
            pltpu.SemaphoreType.DMA((3,)),
            pltpu.SemaphoreType.DMA((SLOTS // 64, 4)),
            pltpu.SemaphoreType.DMA((kinds,)),
            pltpu.SemaphoreType.DMA((kinds,)),
            pltpu.SemaphoreType.DMA((2, N_ROW)),
            pltpu.SemaphoreType.DMA((2, N_COL)),
            pltpu.SemaphoreType.DMA((2, N_ROW)),
            pltpu.SemaphoreType.DMA((2, N_CHIP)),
            pltpu.SemaphoreType.DMA((2,)),
            pltpu.SemaphoreType.DMA((3,)),
            pltpu.SemaphoreType.DMA((3,)),
        ],
        compiler_params=pltpu.CompilerParams(
            collective_id=0, has_side_effects=True, vmem_limit_bytes=58 << 20
        ),
        cost_estimate=pl.CostEstimate(flops=1 << 30, bytes_accessed=9 << 20, transcendentals=0),
    )(block_x, tile_values, row_block, col_block, tile_counts)
    return pl.pallas_call(
        pass_results, out_shape=vectors, in_specs=[vmem] * 3, out_specs=(vmem,) * 3
    )(*results)


def solution(mesh):
    placed = (
        P(("row", "col"), None),
        P("row", "col", None, None),
        P("row", "col", None),
        P("row", "col", None),
        P("row", "col"),
    )
    return jax.shard_map(
        local,
        mesh=mesh,
        in_specs=placed,
        out_specs=(P(("row", "col"), None), P(("row", "col"), None), P()),
        check_vma=False,
    )
```

```python
import functools

import jax
import jax.numpy as jnp
from jax import lax
from jax.experimental import pallas as pl
from jax.experimental.pallas import tpu as pltpu
from jax.sharding import PartitionSpec as P

F32 = jnp.float32
BF16 = jnp.bfloat16
TILE = 64
K = 16
SEGB = 16
SLOTS = 1024
GROUPS = SLOTS // 4
WIDTH = K * TILE
N_ROW = 8
N_COL = 16
N_CHIP = N_COL // 2
RB = N_ROW * SEGB
CB = N_COL * SEGB
STAGE_PITCH = 136
Y_PITCH = 520
EARLY_CHUNKS = 5
HIGHEST = lax.Precision.HIGHEST
NT = (((1,), (1,)), ((), ()))
NN = (((1,), (0,)), ((), ()))


def left_half(rows):
    return lax.broadcasted_iota(jnp.int32, (rows, 128), 1) < TILE


def swap_halves(value):
    return pltpu.roll(value, TILE, 1)


def lane_block(index):
    start = index * 128
    if not isinstance(index, int):
        start = pl.multiple_of(start, 128)
    return pl.ds(start, 128)


def flat_to_by_vector(flat, temp, out):
    lt = left_half(8)

    def step(pair, carry):
        low = flat[0:8, lane_block(pair)]
        high = flat[8:16, lane_block(pair)]
        temp[pl.ds(2 * pair, 8, stride=K), :] = jnp.where(lt, low, swap_halves(high))
        temp[pl.ds(2 * pair + 1, 8, stride=K), :] = jnp.where(lt, swap_halves(low), high)
        return carry

    lax.fori_loop(0, K // 2, step, 0, unroll=True)
    gather_blocks(temp, out)


def gather_blocks(temp, out):
    def step(p, carry):
        out[:, lane_block(p)] = temp[pl.ds(pl.multiple_of(p * K, K), K), :]
        return carry

    lax.fori_loop(0, 8, step, 0, unroll=True)


def by_vector_to_by_row(by_vector, temp, out):
    def spread(p, carry):
        temp[pl.ds(pl.multiple_of(p * K, K), K), :] = by_vector[:, lane_block(p)]
        return carry

    def collect(k, carry):
        out[pl.ds(pl.multiple_of(k * 8, 8), 8), :] = temp[pl.ds(k, 8, stride=K), :]
        return carry

    lax.fori_loop(0, 8, spread, 0, unroll=True)
    lax.fori_loop(0, K, collect, 0, unroll=True)


def by_row_to_flat(by_row, flat):
    lt = left_half(8)

    def step(pair, carry):
        even = by_row[pl.ds(pl.multiple_of(pair * 16, 8), 8), :]
        odd = by_row[pl.ds(pl.multiple_of(pair * 16 + 8, 8), 8), :]
        flat[0:8, lane_block(pair)] = jnp.where(lt, even, swap_halves(odd))
        flat[8:16, lane_block(pair)] = jnp.where(lt, swap_halves(even), odd)
        return carry

    lax.fori_loop(0, K // 2, step, 0, unroll=True)


def load_groups(raw, stage, tiles, chunk, count):
    lt = left_half(16)
    lane_row = lax.broadcasted_iota(jnp.int32, (16, 128), 0)

    def half(a, carry):
        live = [lane_row + ((2 * a + b) * GROUPS + chunk * 16) < count for b in range(2)]

        def step(m, inner):
            first = jnp.where(live[0], raw[chunk, 2 * a, :, lane_block(m)].astype(F32), 0.0)
            second = jnp.where(live[1], raw[chunk, 2 * a + 1, :, lane_block(m)].astype(F32), 0.0)
            even = jnp.where(lt, first, swap_halves(second))
            odd = jnp.where(lt, swap_halves(first), second)
            for h in range(2):
                base = h * 8 * STAGE_PITCH + a * TILE + 2 * m
                stage[pl.ds(base, 8, stride=STAGE_PITCH), :] = even[h * 8 : h * 8 + 8]
                stage[pl.ds(base + 1, 8, stride=STAGE_PITCH), :] = odd[h * 8 : h * 8 + 8]
            return inner

        return lax.fori_loop(0, 32, step, carry, unroll=True)

    lax.fori_loop(0, 2, half, 0, unroll=True)

    def narrow(u, carry):
        tiles[chunk * 16 + u] = stage[pl.ds(pl.multiple_of(u * STAGE_PITCH, 8), 128), :].astype(BF16)
        return carry

    lax.fori_loop(0, 16, narrow, 0, unroll=True)


def fill_table(own, table, base):
    lt = left_half(16)
    zero = jnp.zeros((16, 128), BF16)

    def step(p, carry):
        both = own[:, lane_block(p)]
        turned = swap_halves(both)
        table[base + p, 0] = jnp.where(lt, both, zero)
        table[base + p, 1] = jnp.where(lt, zero, turned)
        table[base + 8 + p, 0] = jnp.where(lt, turned, zero)
        table[base + 8 + p, 1] = jnp.where(lt, zero, both)
        return carry

    lax.fori_loop(0, 8, step, 0, unroll=True)


def multiply(index, table, tiles, products, forward, turned=None):
    lt = left_half(16)

    def step(q, carry):
        picked = [table[index[0, 0, g * GROUPS + q], (g % 2) if forward else (g // 2)] for g in range(4)]
        left = jnp.concatenate(picked, axis=0)
        matrix = tiles[q]
        if turned is not None:
            turned[q] = matrix.T
        out = lax.dot_general(left, matrix, NN, preferred_element_type=F32)
        for s in range(2):
            one, two = (s, 2 + s) if forward else (2 * s, 2 * s + 1)
            merged = jnp.where(lt, out[one * 16 : one * 16 + 16], out[two * 16 : two * 16 + 16])
            place = s * GROUPS + q
            products[pl.ds(place, 8, stride=Y_PITCH), :] = merged[:8]
            products[pl.ds(8 * Y_PITCH + place, 8, stride=Y_PITCH), :] = merged[8:]
        return carry

    lax.fori_loop(0, GROUPS, step, 0, unroll=128)


def add_up(places, products, temp, blocks):
    lt = left_half(8)
    targets = blocks // SEGB

    def step(pair, carry):
        part = [
            products[pl.ds(pl.multiple_of((2 * pair + i) * Y_PITCH, 8), SLOTS // 2), :].astype(BF16) for i in range(2)
        ]
        total = jnp.dot(places[...], jnp.concatenate(part, axis=1), preferred_element_type=F32)
        for target in range(targets):
            for i in range(2):
                half = []
                for h in range(2):
                    first = target * SEGB + h * 8
                    left = total[first : first + 8, i * 128 : i * 128 + 128]
                    right = total[blocks + first : blocks + first + 8, i * 128 : i * 128 + 128]
                    both = jnp.where(lt, left, right)
                    half.append(both + swap_halves(both))
                temp[pl.ds(target * 128 + 2 * pair + i, 8, stride=K), :] = jnp.where(lt, half[0], half[1])
        return carry

    lax.fori_loop(0, K // 2, step, 0, unroll=True)


def narrow_sums(temp, first, stride, out, count):
    def step(target, carry):
        for p in range(8):
            start = (first + target * stride) * 128 + p * K
            out[target, :, p * 128 : p * 128 + 128] = temp[pl.ds(pl.multiple_of(start, K), K), :].astype(BF16)
        return carry

    lax.fori_loop(0, count, step, 0, unroll=True)


def add_pair(temp, first, other, out, count):
    def step(target, carry):
        for p in range(8):
            start = (first + target * 2) * 128 + p * K
            here = temp[pl.ds(pl.multiple_of(start, K), K), :]
            lanes = slice(p * 128, p * 128 + 128)
            out[target, :, lanes] = (here + other[target, :, lanes].astype(F32)).astype(BF16)
        return carry

    lax.fori_loop(0, count, step, 0, unroll=True)


def factor(norm):
    row = lax.broadcasted_iota(jnp.int32, (K, K), 0)
    lane = lax.broadcasted_iota(jnp.int32, (K, K), 1)

    def step(j, carry):
        matrix, inverse = carry
        pivot_row = jnp.sum(jnp.where(row == j, matrix, 0.0), axis=0, keepdims=True)
        pivot_inv = jnp.sum(jnp.where(row == j, inverse, 0.0), axis=0, keepdims=True)
        column = jnp.sum(jnp.where(lane == j, matrix, 0.0), axis=1, keepdims=True)
        pivot = jnp.sum(jnp.where((lane == j) & (row == j), matrix, 0.0), keepdims=True)
        scale = jnp.where(row[:, 0:1] > j, column / pivot, 0.0)
        return matrix - scale * pivot_row, inverse - scale * pivot_inv

    start = (norm, jnp.where(row == lane, 1.0, 0.0).astype(F32))
    matrix, inverse = lax.fori_loop(0, K, step, start)
    diagonal = jnp.sum(jnp.where(row == lane, matrix, 0.0), axis=1, keepdims=True)
    return inverse, 1.0 / diagonal


def kernel(
    block_x, tile_values, row_block, col_block, tile_counts,
    residual_out, image_out, gram_out,
    raw, stage, tiles, turned, table_r, table_c, place_r, place_c, prod_r, prod_c,
    flat_x, row_s, col_s, count_s, row_v, col_v, temp, by_row, vec_x, vec_a, vec_b, gram_last, own, got_r, got_c, part_r, part_c, pair_c, both_c, spare, sum_r, sum_c, gram_own, gram_r, gram_c,
    enter_sem, leave_sem, load_sem, send_r, send_c, recv_r, recv_c, recv_sum_r, recv_sum_c, pair_sem, gram_recv_r, gram_recv_c,
):
    my_row, my_col = lax.axis_index("row"), lax.axis_index("col")
    my_chip, my_core = my_col // 2, lax.rem(my_col, 2)
    sibling = my_chip * 2 + 1 - my_core

    def send(axis, peer, source, target, sent, arrived):
        pltpu.make_async_remote_copy(
            src_ref=source, dst_ref=target, send_sem=sent, recv_sem=arrived,
            device_id={axis: peer}, device_id_type=pl.DeviceIdType.MESH,
        ).start()

    def others(size, me, use):
        def step(d, carry):
            use(lax.rem(me + d, size))
            return carry

        lax.fori_loop(1, size, step, 0, unroll=True)

    def wait_bytes(block, sem):
        pltpu.make_async_copy(block, block, sem).wait()

    def load(chunk, g):
        return pltpu.make_async_copy(
            tile_values.at[0, 0, pl.ds(pl.multiple_of(g * GROUPS + chunk * 16, 16), 16), :],
            raw.at[chunk, g], load_sem.at[chunk, g],
        )

    def start_load(chunk, carry):
        for g in range(4):
            load(chunk, g).start()
        return carry

    barrier = pltpu.get_barrier_semaphore()

    def greet(axis, peer):
        pl.semaphore_signal(barrier, inc=1, device_id={axis: peer}, device_id_type=pl.DeviceIdType.MESH)

    others(N_ROW, my_row, lambda peer: greet("row", peer))
    others(N_COL, my_col, lambda peer: greet("col", peer))

    def put_gram(which, value):
        gram_own[which] = jnp.zeros((8, 128), F32)
        gram_own[which, :, 0:K] = value[0:8]
        gram_own[which, :, K : 2 * K] = value[8:16]

    pairs = (
        (block_x, flat_x), (tile_counts, count_s), (row_block, row_s), (col_block, col_s),
        (row_block, row_v), (col_block, col_v),
    )
    enter = [pltpu.make_async_copy(a, b, enter_sem.at[i]) for i, (a, b) in enumerate(pairs)]

    def leave(which, source, target):
        return pltpu.make_async_copy(source, target, leave_sem.at[which])

    for arrival in enter:
        arrival.start()
    lax.fori_loop(0, SLOTS // 64, start_load, 0)
    enter[0].wait()
    flat_to_by_vector(flat_x, temp, vec_x)
    own[0] = vec_x[...].astype(BF16)
    norm = lax.dot_general(vec_x[...], vec_x[...], NT, precision=HIGHEST, preferred_element_type=F32)
    put_gram(0, norm)
    enter[1].wait()
    count = count_s[0, 0]

    def arrange(chunk, carry):
        for g in range(4):
            load(chunk, g).wait()
        load_groups(raw, stage, tiles, chunk, count)
        return carry

    lax.fori_loop(0, EARLY_CHUNKS, arrange, 0)
    pl.semaphore_wait(barrier, N_ROW + N_COL - 2)

    def gather(step, beside):
        def to_row(peer):
            send("row", peer, own.at[step], got_r.at[step, my_row], send_r.at[step], recv_r.at[step, my_row])

        def to_col(peer):
            send(
                "col", peer, own.at[step], got_c.at[step, my_chip, my_core], send_c.at[step], recv_c.at[step, my_col]
            )

        others(N_ROW, my_row, to_row)
        others(N_CHIP, my_chip, lambda chip: to_col(chip * 2 + my_core))
        to_col(sibling)
        got_c[step, my_chip, my_core] = own[step]
        beside()

    def forward(step):
        def pass_on(chip):
            slot = chip * 2 + my_core
            block = got_c.at[step, chip, my_core]
            wait_bytes(block, recv_c.at[step, slot])
            send("col", sibling, block, block, send_c.at[step], recv_c.at[step, slot])

        others(N_CHIP, my_chip, pass_on)

    def gram_row(which):
        def to_row(peer):
            send(
                "row", peer, gram_own.at[which], gram_r.at[which, my_row], send_r.at[4 + which], gram_recv_r.at[which]
            )

        others(N_ROW, my_row, to_row)
        gram_r[which, my_row] = gram_own[which]

    def gram_col(which):
        wait_bytes(gram_r.at[which, pl.ds(0, N_ROW - 1)], gram_recv_r.at[which])
        gram_own[3 + which] = jnp.sum(gram_r[which], axis=0)

        def to_col(peer):
            send(
                "col", peer, gram_own.at[3 + which], gram_c.at[which, my_col], send_c.at[4 + which],
                gram_recv_c.at[which],
            )

        others(N_COL, my_col, to_col)
        gram_c[which, my_col] = gram_own[3 + which]

    def gram_done(which):
        wait_bytes(gram_c.at[which, pl.ds(0, N_COL - 1)], gram_recv_c.at[which])
        total = jnp.sum(gram_c[which], axis=0)
        return jnp.concatenate([total[:, 0:K], total[:, K : 2 * K]], axis=0)

    def cross_part(step):
        total = jnp.zeros((K, K), F32)
        for side in range(2):
            core = my_core if side == 0 else 1 - my_core
            sums = part_c[step, side].reshape(N_CHIP * K, WIDTH)
            vectors = got_c[step, :, core].reshape(N_CHIP * K, WIDTH)
            pairs = lax.dot_general(sums, vectors, NT, preferred_element_type=F32)
            for chip in range(N_CHIP):
                total += pairs[chip * K : chip * K + K, chip * K : chip * K + K]
        return total

    def fill_all(step):
        def enter(chip, carry):
            for core in range(2):
                fill_table(got_c.at[step, chip, core], table_c, (chip * 2 + core) * SEGB)
            return carry

        lax.fori_loop(0, N_CHIP, enter, 0, unroll=4)

    def finish_sends(step):
        sent_c = spare.at[pl.ds(0, N_COL - 1)]
        wait_bytes(got_r.at[step, pl.ds(0, N_ROW - 1)], send_r.at[step])
        wait_bytes(sent_c, send_c.at[step])
        wait_bytes(got_r.at[step, pl.ds(0, N_ROW - 1)], send_r.at[2 + step])
        wait_bytes(sent_c, send_c.at[2 + step])
        for which in (0, 1) if step == 0 else (2,):
            wait_bytes(gram_r.at[which, pl.ds(0, N_ROW - 1)], send_r.at[4 + which])
            wait_bytes(gram_c.at[which, pl.ds(0, N_COL - 1)], send_c.at[4 + which])

    def arrange_rest():
        gram_row(0)
        lax.fori_loop(EARLY_CHUNKS, SLOTS // 64, arrange, 0)

    gather(0, arrange_rest)
    for arrival in enter[2:]:
        arrival.wait()
    for s in range(2):
        columns = jnp.concatenate(
            [col_v[0, :, s * 256 : s * 256 + 256], col_v[0, :, 512 + s * 256 : 768 + s * 256]], axis=1
        )
        hit = lax.broadcasted_iota(jnp.int32, (CB, 512), 0) == columns
        place_c[s * CB : s * CB + CB, :] = jnp.where(hit, 1.0, 0.0).astype(BF16)
        hit = lax.broadcasted_iota(jnp.int32, (RB, 512), 0) == row_v[0, :, s * 512 : s * 512 + 512]
        place_r[s * RB : s * RB + RB, :] = jnp.where(hit, 1.0, 0.0).astype(BF16)
    gram_col(0)

    def product(step):
        def arrive_row(peer):
            wait_bytes(got_r.at[step, peer], recv_r.at[step, peer])

        def enter_row(d, carry):
            peer = lax.rem(my_row + d, N_ROW)
            fill_table(got_r.at[step, peer], table_r, peer * SEGB)
            return carry

        def arrive_other(chip):
            wait_bytes(got_c.at[step, chip, 1 - my_core], recv_c.at[step, chip * 2 + 1 - my_core])

        fill_table(own.at[step], table_r, my_row * SEGB)
        others(N_ROW, my_row, arrive_row)
        lax.fori_loop(1, N_ROW, enter_row, 0, unroll=True)
        multiply(row_s, table_r, tiles, prod_c, False, turned if step == 0 else None)
        forward(step)
        add_up(place_c, prod_c, temp, CB)
        narrow_sums(temp, 1 - my_core, 2, part_c.at[step, 1], N_CHIP)
        send("col", sibling, part_c.at[step, 1], pair_c.at[step], send_c.at[2 + step], pair_sem.at[step])
        narrow_sums(temp, my_core, 2, part_c.at[step, 0], N_CHIP)
        arrive_other(my_chip)
        others(N_CHIP, my_chip, arrive_other)
        put_gram(1 + step, cross_part(step))
        gram_row(1 + step)
        fill_all(step)
        wait_bytes(pair_c.at[step], pair_sem.at[step])
        add_pair(temp, my_core, pair_c.at[step], both_c.at[step], N_CHIP)

        def sums_to_col(chip):
            send(
                "col", chip * 2 + my_core, both_c.at[step, chip], sum_c.at[step, my_chip], send_c.at[2 + step],
                recv_sum_c.at[step, my_chip],
            )

        others(N_CHIP, my_chip, sums_to_col)
        multiply(col_s, table_c, turned, prod_r, True)
        gram_col(1 + step)
        add_up(place_r, prod_r, temp, RB)
        narrow_sums(temp, 0, 1, part_r.at[step], N_ROW)

        def sums_to_row(peer):
            send(
                "row", peer, part_r.at[step, peer], sum_r.at[step, my_row], send_r.at[2 + step],
                recv_sum_r.at[step, my_row],
            )

        others(N_ROW, my_row, sums_to_row)
        if step == 0:
            inverse, scale = factor(gram_done(0))
            norm_inverse = lax.dot_general(
                inverse * scale, inverse, (((0,), (0,)), ((), ())), precision=HIGHEST, preferred_element_type=F32
            )

        def add_col(chip):
            wait_bytes(sum_c.at[step, chip], recv_sum_c.at[step, chip])
            vec_a[...] += sum_c[step, chip].astype(F32)

        vec_a[...] = both_c[step, my_chip].astype(F32) + part_r[step, my_row].astype(F32)
        others(N_CHIP, my_chip, add_col)
        half = gram_done(1 + step)
        cross = half + half.T
        if step == 0:
            coupling = jnp.dot(cross, norm_inverse, precision=HIGHEST, preferred_element_type=F32)
            vec_a[...] -= jnp.dot(coupling, vec_x[...], precision=HIGHEST, preferred_element_type=F32)

        def arrive_sum(peer):
            wait_bytes(sum_r.at[step, peer], recv_sum_r.at[step, peer])

        others(N_ROW, my_row, arrive_sum)
        sum_r[step, my_row] = jnp.zeros((K, WIDTH), BF16)

        def add_row(p, carry):
            total = vec_a[:, lane_block(p)]
            for slot in range(N_ROW):
                total += sum_r[step, slot, :, lane_block(p)].astype(F32)
            vec_a[:, lane_block(p)] = total
            if step == 0:
                own[1, :, lane_block(p)] = total.astype(BF16)
            return carry

        lax.fori_loop(0, 8, add_row, 0, unroll=True)
        return cross

    product(0)

    def keep_residual():
        by_vector_to_by_row(vec_a, temp, by_row)
        by_row_to_flat(by_row, vec_x)
        leave(0, vec_x, residual_out).start()
        finish_sends(0)

    gather(1, keep_residual)
    last = product(1)
    by_vector_to_by_row(vec_a, temp, by_row)
    by_row_to_flat(by_row, vec_b)
    gram_last[...] = last * (1.0 / (N_ROW * N_COL * SEGB * TILE))
    leave(1, vec_b, image_out).start()
    leave(2, gram_last, gram_out).start()
    finish_sends(1)
    leave(0, vec_x, residual_out).wait()
    leave(1, vec_b, image_out).wait()
    leave(2, gram_last, gram_out).wait()


def pass_results(residual, image, gram, residual_out, image_out, gram_out):
    residual_out[...] = residual[...]
    image_out[...] = image[...]
    gram_out[...] = gram[...]


def local(block_x, tile_values, row_block, col_block, tile_counts):
    vmem = pl.BlockSpec(memory_space=pltpu.VMEM)
    anywhere = pl.BlockSpec(memory_space=pl.ANY)
    kinds = 7
    vectors = (
        jax.ShapeDtypeStruct((SEGB, WIDTH), F32),
        jax.ShapeDtypeStruct((SEGB, WIDTH), F32),
        jax.ShapeDtypeStruct((K, K), F32),
    )
    results = pl.pallas_call(
        kernel,
        out_shape=vectors,
        in_specs=[anywhere] * 5,
        out_specs=(anywhere,) * 3,
        scratch_shapes=[
            pltpu.VMEM((SLOTS // 64, 4, 16, TILE * TILE), BF16),
            pltpu.VMEM((16 * STAGE_PITCH, 128), F32),
            pltpu.VMEM((GROUPS, 128, 128), BF16),
            pltpu.VMEM((GROUPS, 128, 128), BF16),
            pltpu.VMEM((RB, 2, K, 128), BF16),
            pltpu.VMEM((CB, 2, K, 128), BF16),
            pltpu.VMEM((2 * RB, 512), BF16),
            pltpu.VMEM((2 * CB, 512), BF16),
            pltpu.VMEM((K * Y_PITCH, 128), F32),
            pltpu.VMEM((K * Y_PITCH, 128), F32),
            pltpu.VMEM((SEGB, WIDTH), F32),
            pltpu.SMEM((1, 1, SLOTS), jnp.int32),
            pltpu.SMEM((1, 1, SLOTS), jnp.int32),
            pltpu.SMEM((1, 1), jnp.int32),
            pltpu.VMEM((1, 1, SLOTS), jnp.int32),
            pltpu.VMEM((1, 1, SLOTS), jnp.int32),
            pltpu.VMEM((N_COL * 128, 128), F32),
            pltpu.VMEM((128, 128), F32),
            pltpu.VMEM((K, WIDTH), F32),
            pltpu.VMEM((K, WIDTH), F32),
            pltpu.VMEM((K, WIDTH), F32),
            pltpu.VMEM((K, K), F32),
            pltpu.VMEM((2, K, WIDTH), BF16),
            pltpu.VMEM((2, N_ROW, K, WIDTH), BF16),
            pltpu.VMEM((2, N_CHIP, 2, K, WIDTH), BF16),
            pltpu.VMEM((2, N_ROW, K, WIDTH), BF16),
            pltpu.VMEM((2, 2, N_CHIP, K, WIDTH), BF16),
            pltpu.VMEM((2, N_CHIP, K, WIDTH), BF16),
            pltpu.VMEM((2, N_CHIP, K, WIDTH), BF16),
            pltpu.VMEM((N_COL, K, WIDTH), BF16),
            pltpu.VMEM((2, N_ROW, K, WIDTH), BF16),
            pltpu.VMEM((2, N_CHIP, K, WIDTH), BF16),
            pltpu.VMEM((6, 8, 128), F32),
            pltpu.VMEM((3, N_ROW, 8, 128), F32),
            pltpu.VMEM((3, N_COL, 8, 128), F32),
            pltpu.SemaphoreType.DMA((6,)),
            pltpu.SemaphoreType.DMA((3,)),
            pltpu.SemaphoreType.DMA((SLOTS // 64, 4)),
            pltpu.SemaphoreType.DMA((kinds,)),
            pltpu.SemaphoreType.DMA((kinds,)),
            pltpu.SemaphoreType.DMA((2, N_ROW)),
            pltpu.SemaphoreType.DMA((2, N_COL)),
            pltpu.SemaphoreType.DMA((2, N_ROW)),
            pltpu.SemaphoreType.DMA((2, N_CHIP)),
            pltpu.SemaphoreType.DMA((2,)),
            pltpu.SemaphoreType.DMA((3,)),
            pltpu.SemaphoreType.DMA((3,)),
        ],
        compiler_params=pltpu.CompilerParams(
            collective_id=0, has_side_effects=True, vmem_limit_bytes=58 << 20
        ),
        cost_estimate=pl.CostEstimate(flops=1 << 30, bytes_accessed=9 << 20, transcendentals=0),
    )(block_x, tile_values, row_block, col_block, tile_counts)
    return pl.pallas_call(
        pass_results, out_shape=vectors, in_specs=[vmem] * 3, out_specs=(vmem,) * 3
    )(*results)


def solution(mesh):
    placed = (
        P(("row", "col"), None),
        P("row", "col", None, None),
        P("row", "col", None),
        P("row", "col", None),
        P("row", "col"),
    )
    return jax.shard_map(
        local,
        mesh=mesh,
        in_specs=placed,
        out_specs=(P(("row", "col"), None), P(("row", "col"), None), P()),
        check_vma=False,
    )
```

```python
import functools

import jax
import jax.numpy as jnp
from jax import lax
from jax.experimental import pallas as pl
from jax.experimental.pallas import tpu as pltpu
from jax.sharding import PartitionSpec as P

F32 = jnp.float32
BF16 = jnp.bfloat16
TILE = 64
K = 16
SEGB = 16
SLOTS = 1024
GROUPS = SLOTS // 4
WIDTH = K * TILE
N_ROW = 8
N_COL = 16
N_CHIP = N_COL // 2
RB = N_ROW * SEGB
CB = N_COL * SEGB
STAGE_PITCH = 136
Y_PITCH = 520
EARLY_CHUNKS = 3
HIGHEST = lax.Precision.HIGHEST
NT = (((1,), (1,)), ((), ()))
NN = (((1,), (0,)), ((), ()))


def left_half(rows):
    return lax.broadcasted_iota(jnp.int32, (rows, 128), 1) < TILE


def swap_halves(value):
    return pltpu.roll(value, TILE, 1)


def lane_block(index):
    start = index * 128
    if not isinstance(index, int):
        start = pl.multiple_of(start, 128)
    return pl.ds(start, 128)


def flat_to_by_vector(flat, temp, out):
    lt = left_half(8)

    def step(pair, carry):
        low = flat[0:8, lane_block(pair)]
        high = flat[8:16, lane_block(pair)]
        temp[pl.ds(2 * pair, 8, stride=K), :] = jnp.where(lt, low, swap_halves(high))
        temp[pl.ds(2 * pair + 1, 8, stride=K), :] = jnp.where(lt, swap_halves(low), high)
        return carry

    lax.fori_loop(0, K // 2, step, 0, unroll=True)
    gather_blocks(temp, out)


def gather_blocks(temp, out):
    def step(p, carry):
        out[:, lane_block(p)] = temp[pl.ds(pl.multiple_of(p * K, K), K), :]
        return carry

    lax.fori_loop(0, 8, step, 0, unroll=True)


def by_vector_to_by_row(by_vector, temp, out):
    def spread(p, carry):
        temp[pl.ds(pl.multiple_of(p * K, K), K), :] = by_vector[:, lane_block(p)]
        return carry

    def collect(k, carry):
        out[pl.ds(pl.multiple_of(k * 8, 8), 8), :] = temp[pl.ds(k, 8, stride=K), :]
        return carry

    lax.fori_loop(0, 8, spread, 0, unroll=True)
    lax.fori_loop(0, K, collect, 0, unroll=True)


def by_row_to_flat(by_row, flat):
    lt = left_half(8)

    def step(pair, carry):
        even = by_row[pl.ds(pl.multiple_of(pair * 16, 8), 8), :]
        odd = by_row[pl.ds(pl.multiple_of(pair * 16 + 8, 8), 8), :]
        flat[0:8, lane_block(pair)] = jnp.where(lt, even, swap_halves(odd))
        flat[8:16, lane_block(pair)] = jnp.where(lt, swap_halves(even), odd)
        return carry

    lax.fori_loop(0, K // 2, step, 0, unroll=True)


def load_groups(raw, stage, tiles, chunk, count):
    lt = left_half(16)
    lane_row = lax.broadcasted_iota(jnp.int32, (16, 128), 0)

    def half(a, carry):
        live = [lane_row + ((2 * a + b) * GROUPS + chunk * 16) < count for b in range(2)]

        def step(m, inner):
            first = jnp.where(live[0], raw[chunk, 2 * a, :, lane_block(m)].astype(F32), 0.0)
            second = jnp.where(live[1], raw[chunk, 2 * a + 1, :, lane_block(m)].astype(F32), 0.0)
            even = jnp.where(lt, first, swap_halves(second))
            odd = jnp.where(lt, swap_halves(first), second)
            for h in range(2):
                base = h * 8 * STAGE_PITCH + a * TILE + 2 * m
                stage[pl.ds(base, 8, stride=STAGE_PITCH), :] = even[h * 8 : h * 8 + 8]
                stage[pl.ds(base + 1, 8, stride=STAGE_PITCH), :] = odd[h * 8 : h * 8 + 8]
            return inner

        return lax.fori_loop(0, 32, step, carry, unroll=True)

    lax.fori_loop(0, 2, half, 0, unroll=True)

    def narrow(u, carry):
        tiles[chunk * 16 + u] = stage[pl.ds(pl.multiple_of(u * STAGE_PITCH, 8), 128), :].astype(BF16)
        return carry

    lax.fori_loop(0, 16, narrow, 0, unroll=True)


def fill_table(own, table, base):
    lt = left_half(16)
    zero = jnp.zeros((16, 128), BF16)

    def step(p, carry):
        both = own[:, lane_block(p)]
        turned = swap_halves(both)
        table[base + p, 0] = jnp.where(lt, both, zero)
        table[base + p, 1] = jnp.where(lt, zero, turned)
        table[base + 8 + p, 0] = jnp.where(lt, turned, zero)
        table[base + 8 + p, 1] = jnp.where(lt, zero, both)
        return carry

    lax.fori_loop(0, 8, step, 0, unroll=True)


def multiply(index, table, tiles, products, forward, turned=None):
    lt = left_half(16)

    def step(q, carry):
        picked = [table[index[0, 0, g * GROUPS + q], (g % 2) if forward else (g // 2)] for g in range(4)]
        left = jnp.concatenate(picked, axis=0)
        matrix = tiles[q]
        if turned is not None:
            turned[q] = matrix.T
        out = lax.dot_general(left, matrix, NN, preferred_element_type=F32)
        for s in range(2):
            one, two = (s, 2 + s) if forward else (2 * s, 2 * s + 1)
            merged = jnp.where(lt, out[one * 16 : one * 16 + 16], out[two * 16 : two * 16 + 16])
            place = s * GROUPS + q
            products[pl.ds(place, 8, stride=Y_PITCH), :] = merged[:8]
            products[pl.ds(8 * Y_PITCH + place, 8, stride=Y_PITCH), :] = merged[8:]
        return carry

    lax.fori_loop(0, GROUPS, step, 0, unroll=128)


def add_up(places, products, temp, blocks):
    lt = left_half(8)
    targets = blocks // SEGB

    def step(pair, carry):
        part = [
            products[pl.ds(pl.multiple_of((2 * pair + i) * Y_PITCH, 8), SLOTS // 2), :].astype(BF16) for i in range(2)
        ]
        total = jnp.dot(places[...], jnp.concatenate(part, axis=1), preferred_element_type=F32)
        for target in range(targets):
            for i in range(2):
                half = []
                for h in range(2):
                    first = target * SEGB + h * 8
                    left = total[first : first + 8, i * 128 : i * 128 + 128]
                    right = total[blocks + first : blocks + first + 8, i * 128 : i * 128 + 128]
                    both = jnp.where(lt, left, right)
                    half.append(both + swap_halves(both))
                temp[pl.ds(target * 128 + 2 * pair + i, 8, stride=K), :] = jnp.where(lt, half[0], half[1])
        return carry

    lax.fori_loop(0, K // 2, step, 0, unroll=True)


def narrow_sums(temp, first, stride, out, count):
    def step(target, carry):
        for p in range(8):
            start = (first + target * stride) * 128 + p * K
            out[target, :, p * 128 : p * 128 + 128] = temp[pl.ds(pl.multiple_of(start, K), K), :].astype(BF16)
        return carry

    lax.fori_loop(0, count, step, 0, unroll=True)


def add_pair(temp, first, other, out, count):
    def step(target, carry):
        for p in range(8):
            start = (first + target * 2) * 128 + p * K
            here = temp[pl.ds(pl.multiple_of(start, K), K), :]
            lanes = slice(p * 128, p * 128 + 128)
            out[target, :, lanes] = (here + other[target, :, lanes].astype(F32)).astype(BF16)
        return carry

    lax.fori_loop(0, count, step, 0, unroll=True)


def factor(norm):
    row = lax.broadcasted_iota(jnp.int32, (K, K), 0)
    lane = lax.broadcasted_iota(jnp.int32, (K, K), 1)

    def step(j, carry):
        matrix, inverse = carry
        pivot_row = jnp.sum(jnp.where(row == j, matrix, 0.0), axis=0, keepdims=True)
        pivot_inv = jnp.sum(jnp.where(row == j, inverse, 0.0), axis=0, keepdims=True)
        column = jnp.sum(jnp.where(lane == j, matrix, 0.0), axis=1, keepdims=True)
        pivot = jnp.sum(jnp.where((lane == j) & (row == j), matrix, 0.0), keepdims=True)
        scale = jnp.where(row[:, 0:1] > j, column / pivot, 0.0)
        return matrix - scale * pivot_row, inverse - scale * pivot_inv

    start = (norm, jnp.where(row == lane, 1.0, 0.0).astype(F32))
    matrix, inverse = lax.fori_loop(0, K, step, start)
    diagonal = jnp.sum(jnp.where(row == lane, matrix, 0.0), axis=1, keepdims=True)
    return inverse, 1.0 / diagonal


def kernel(
    block_x, tile_values, row_block, col_block, tile_counts,
    residual_out, image_out, gram_out,
    raw, stage, tiles, turned, table_r, table_c, place_r, place_c, prod_r, prod_c,
    flat_x, row_s, col_s, count_s, row_v, col_v, temp, by_row, vec_x, vec_a, vec_b, gram_last, own, got_r, got_c, part_r, part_c, pair_c, both_c, spare, sum_r, sum_c, gram_own, gram_r, gram_c,
    enter_sem, leave_sem, load_sem, send_r, send_c, recv_r, recv_c, recv_sum_r, recv_sum_c, pair_sem, gram_recv_r, gram_recv_c,
):
    my_row, my_col = lax.axis_index("row"), lax.axis_index("col")
    my_chip, my_core = my_col // 2, lax.rem(my_col, 2)
    sibling = my_chip * 2 + 1 - my_core

    def send(axis, peer, source, target, sent, arrived):
        pltpu.make_async_remote_copy(
            src_ref=source, dst_ref=target, send_sem=sent, recv_sem=arrived,
            device_id={axis: peer}, device_id_type=pl.DeviceIdType.MESH,
        ).start()

    def others(size, me, use):
        def step(d, carry):
            use(lax.rem(me + d, size))
            return carry

        lax.fori_loop(1, size, step, 0, unroll=True)

    def wait_bytes(block, sem):
        pltpu.make_async_copy(block, block, sem).wait()

    def load(chunk, g):
        return pltpu.make_async_copy(
            tile_values.at[0, 0, pl.ds(pl.multiple_of(g * GROUPS + chunk * 16, 16), 16), :],
            raw.at[chunk, g], load_sem.at[chunk, g],
        )

    def start_load(chunk, carry):
        for g in range(4):
            load(chunk, g).start()
        return carry

    barrier = pltpu.get_barrier_semaphore()

    def greet(axis, peer):
        pl.semaphore_signal(barrier, inc=1, device_id={axis: peer}, device_id_type=pl.DeviceIdType.MESH)

    others(N_ROW, my_row, lambda peer: greet("row", peer))
    others(N_COL, my_col, lambda peer: greet("col", peer))

    def put_gram(which, value):
        gram_own[which] = jnp.zeros((8, 128), F32)
        gram_own[which, :, 0:K] = value[0:8]
        gram_own[which, :, K : 2 * K] = value[8:16]

    pairs = (
        (block_x, flat_x), (tile_counts, count_s), (row_block, row_s), (col_block, col_s),
        (row_block, row_v), (col_block, col_v),
    )
    enter = [pltpu.make_async_copy(a, b, enter_sem.at[i]) for i, (a, b) in enumerate(pairs)]

    def leave(which, source, target):
        return pltpu.make_async_copy(source, target, leave_sem.at[which])

    for arrival in enter:
        arrival.start()
    lax.fori_loop(0, SLOTS // 64, start_load, 0)
    enter[0].wait()
    flat_to_by_vector(flat_x, temp, vec_x)
    own[0] = vec_x[...].astype(BF16)
    norm = lax.dot_general(vec_x[...], vec_x[...], NT, precision=HIGHEST, preferred_element_type=F32)
    put_gram(0, norm)
    enter[1].wait()
    count = count_s[0, 0]

    def arrange(chunk, carry):
        for g in range(4):
            load(chunk, g).wait()
        load_groups(raw, stage, tiles, chunk, count)
        return carry

    for arrival in enter[2:]:
        arrival.wait()
    for s in range(2):
        columns = jnp.concatenate(
            [col_v[0, :, s * 256 : s * 256 + 256], col_v[0, :, 512 + s * 256 : 768 + s * 256]], axis=1
        )
        hit = lax.broadcasted_iota(jnp.int32, (CB, 512), 0) == columns
        place_c[s * CB : s * CB + CB, :] = jnp.where(hit, 1.0, 0.0).astype(BF16)
        hit = lax.broadcasted_iota(jnp.int32, (RB, 512), 0) == row_v[0, :, s * 512 : s * 512 + 512]
        place_r[s * RB : s * RB + RB, :] = jnp.where(hit, 1.0, 0.0).astype(BF16)
    lax.fori_loop(0, EARLY_CHUNKS, arrange, 0)
    pl.semaphore_wait(barrier, N_ROW + N_COL - 2)

    def gather(step, beside):
        def to_row(peer):
            send("row", peer, own.at[step], got_r.at[step, my_row], send_r.at[step], recv_r.at[step, my_row])

        def to_col(peer):
            send(
                "col", peer, own.at[step], got_c.at[step, my_chip, my_core], send_c.at[step], recv_c.at[step, my_col]
            )

        others(N_ROW, my_row, to_row)
        others(N_CHIP, my_chip, lambda chip: to_col(chip * 2 + my_core))
        to_col(sibling)
        got_c[step, my_chip, my_core] = own[step]
        beside()

    def forward(step):
        def pass_on(chip):
            slot = chip * 2 + my_core
            block = got_c.at[step, chip, my_core]
            wait_bytes(block, recv_c.at[step, slot])
            send("col", sibling, block, block, send_c.at[step], recv_c.at[step, slot])

        others(N_CHIP, my_chip, pass_on)

    def gram_row(which):
        def to_row(peer):
            send(
                "row", peer, gram_own.at[which], gram_r.at[which, my_row], send_r.at[4 + which], gram_recv_r.at[which]
            )

        others(N_ROW, my_row, to_row)
        gram_r[which, my_row] = gram_own[which]

    def gram_col(which):
        wait_bytes(gram_r.at[which, pl.ds(0, N_ROW - 1)], gram_recv_r.at[which])
        gram_own[3 + which] = jnp.sum(gram_r[which], axis=0)

        def to_col(peer):
            send(
                "col", peer, gram_own.at[3 + which], gram_c.at[which, my_col], send_c.at[4 + which],
                gram_recv_c.at[which],
            )

        others(N_COL, my_col, to_col)
        gram_c[which, my_col] = gram_own[3 + which]

    def gram_done(which):
        wait_bytes(gram_c.at[which, pl.ds(0, N_COL - 1)], gram_recv_c.at[which])
        total = jnp.sum(gram_c[which], axis=0)
        return jnp.concatenate([total[:, 0:K], total[:, K : 2 * K]], axis=0)

    def cross_part(step):
        total = jnp.zeros((K, K), F32)
        for side in range(2):
            core = my_core if side == 0 else 1 - my_core
            sums = part_c[step, side].reshape(N_CHIP * K, WIDTH)
            vectors = got_c[step, :, core].reshape(N_CHIP * K, WIDTH)
            pairs = lax.dot_general(sums, vectors, NT, preferred_element_type=F32)
            for chip in range(N_CHIP):
                total += pairs[chip * K : chip * K + K, chip * K : chip * K + K]
        return total

    def fill_all(step):
        def enter(chip, carry):
            for core in range(2):
                fill_table(got_c.at[step, chip, core], table_c, (chip * 2 + core) * SEGB)
            return carry

        lax.fori_loop(0, N_CHIP, enter, 0, unroll=4)

    def finish_sends(step):
        sent_c = spare.at[pl.ds(0, N_COL - 1)]
        wait_bytes(got_r.at[step, pl.ds(0, N_ROW - 1)], send_r.at[step])
        wait_bytes(sent_c, send_c.at[step])
        wait_bytes(got_r.at[step, pl.ds(0, N_ROW - 1)], send_r.at[2 + step])
        wait_bytes(sent_c, send_c.at[2 + step])
        for which in (0, 1) if step == 0 else (2,):
            wait_bytes(gram_r.at[which, pl.ds(0, N_ROW - 1)], send_r.at[4 + which])
            wait_bytes(gram_c.at[which, pl.ds(0, N_COL - 1)], send_c.at[4 + which])

    def arrange_rest():
        gram_row(0)
        lax.fori_loop(EARLY_CHUNKS, SLOTS // 64, arrange, 0)

    gather(0, arrange_rest)
    gram_col(0)

    def product(step):
        def arrive_row(peer):
            wait_bytes(got_r.at[step, peer], recv_r.at[step, peer])

        def enter_row(d, carry):
            peer = lax.rem(my_row + d, N_ROW)
            fill_table(got_r.at[step, peer], table_r, peer * SEGB)
            return carry

        def arrive_other(chip):
            wait_bytes(got_c.at[step, chip, 1 - my_core], recv_c.at[step, chip * 2 + 1 - my_core])

        fill_table(own.at[step], table_r, my_row * SEGB)
        others(N_ROW, my_row, arrive_row)
        lax.fori_loop(1, N_ROW, enter_row, 0, unroll=True)
        multiply(row_s, table_r, tiles, prod_c, False, turned if step == 0 else None)
        forward(step)
        add_up(place_c, prod_c, temp, CB)
        narrow_sums(temp, 1 - my_core, 2, part_c.at[step, 1], N_CHIP)
        send("col", sibling, part_c.at[step, 1], pair_c.at[step], send_c.at[2 + step], pair_sem.at[step])
        narrow_sums(temp, my_core, 2, part_c.at[step, 0], N_CHIP)
        arrive_other(my_chip)
        others(N_CHIP, my_chip, arrive_other)
        put_gram(1 + step, cross_part(step))
        gram_row(1 + step)
        fill_all(step)
        wait_bytes(pair_c.at[step], pair_sem.at[step])
        add_pair(temp, my_core, pair_c.at[step], both_c.at[step], N_CHIP)

        def sums_to_col(chip):
            send(
                "col", chip * 2 + my_core, both_c.at[step, chip], sum_c.at[step, my_chip], send_c.at[2 + step],
                recv_sum_c.at[step, my_chip],
            )

        others(N_CHIP, my_chip, sums_to_col)
        multiply(col_s, table_c, turned, prod_r, True)
        gram_col(1 + step)
        add_up(place_r, prod_r, temp, RB)
        narrow_sums(temp, 0, 1, part_r.at[step], N_ROW)

        def sums_to_row(peer):
            send(
                "row", peer, part_r.at[step, peer], sum_r.at[step, my_row], send_r.at[2 + step],
                recv_sum_r.at[step, my_row],
            )

        others(N_ROW, my_row, sums_to_row)
        if step == 0:
            inverse, scale = factor(gram_done(0))
            norm_inverse = lax.dot_general(
                inverse * scale, inverse, (((0,), (0,)), ((), ())), precision=HIGHEST, preferred_element_type=F32
            )

        def add_col(chip):
            wait_bytes(sum_c.at[step, chip], recv_sum_c.at[step, chip])
            vec_a[...] += sum_c[step, chip].astype(F32)

        vec_a[...] = both_c[step, my_chip].astype(F32) + part_r[step, my_row].astype(F32)
        others(N_CHIP, my_chip, add_col)
        half = gram_done(1 + step)
        cross = half + half.T
        if step == 0:
            coupling = jnp.dot(cross, norm_inverse, precision=HIGHEST, preferred_element_type=F32)
            vec_a[...] -= jnp.dot(coupling, vec_x[...], precision=HIGHEST, preferred_element_type=F32)

        def arrive_sum(peer):
            wait_bytes(sum_r.at[step, peer], recv_sum_r.at[step, peer])

        others(N_ROW, my_row, arrive_sum)
        sum_r[step, my_row] = jnp.zeros((K, WIDTH), BF16)

        def add_row(p, carry):
            total = vec_a[:, lane_block(p)]
            for slot in range(N_ROW):
                total += sum_r[step, slot, :, lane_block(p)].astype(F32)
            vec_a[:, lane_block(p)] = total
            if step == 0:
                own[1, :, lane_block(p)] = total.astype(BF16)
            return carry

        lax.fori_loop(0, 8, add_row, 0, unroll=True)
        return cross

    product(0)

    def keep_residual():
        by_vector_to_by_row(vec_a, temp, by_row)
        by_row_to_flat(by_row, vec_x)
        leave(0, vec_x, residual_out).start()
        finish_sends(0)

    gather(1, keep_residual)
    last = product(1)
    by_vector_to_by_row(vec_a, temp, by_row)
    by_row_to_flat(by_row, vec_b)
    gram_last[...] = last * (1.0 / (N_ROW * N_COL * SEGB * TILE))
    leave(1, vec_b, image_out).start()
    leave(2, gram_last, gram_out).start()
    finish_sends(1)
    leave(0, vec_x, residual_out).wait()
    leave(1, vec_b, image_out).wait()
    leave(2, gram_last, gram_out).wait()


def pass_results(residual, image, gram, residual_out, image_out, gram_out):
    residual_out[...] = residual[...]
    image_out[...] = image[...]
    gram_out[...] = gram[...]


def local(block_x, tile_values, row_block, col_block, tile_counts):
    vmem = pl.BlockSpec(memory_space=pltpu.VMEM)
    anywhere = pl.BlockSpec(memory_space=pl.ANY)
    kinds = 7
    vectors = (
        jax.ShapeDtypeStruct((SEGB, WIDTH), F32),
        jax.ShapeDtypeStruct((SEGB, WIDTH), F32),
        jax.ShapeDtypeStruct((K, K), F32),
    )
    results = pl.pallas_call(
        kernel,
        out_shape=vectors,
        in_specs=[anywhere] * 5,
        out_specs=(anywhere,) * 3,
        scratch_shapes=[
            pltpu.VMEM((SLOTS // 64, 4, 16, TILE * TILE), BF16),
            pltpu.VMEM((16 * STAGE_PITCH, 128), F32),
            pltpu.VMEM((GROUPS, 128, 128), BF16),
            pltpu.VMEM((GROUPS, 128, 128), BF16),
            pltpu.VMEM((RB, 2, K, 128), BF16),
            pltpu.VMEM((CB, 2, K, 128), BF16),
            pltpu.VMEM((2 * RB, 512), BF16),
            pltpu.VMEM((2 * CB, 512), BF16),
            pltpu.VMEM((K * Y_PITCH, 128), F32),
            pltpu.VMEM((K * Y_PITCH, 128), F32),
            pltpu.VMEM((SEGB, WIDTH), F32),
            pltpu.SMEM((1, 1, SLOTS), jnp.int32),
            pltpu.SMEM((1, 1, SLOTS), jnp.int32),
            pltpu.SMEM((1, 1), jnp.int32),
            pltpu.VMEM((1, 1, SLOTS), jnp.int32),
            pltpu.VMEM((1, 1, SLOTS), jnp.int32),
            pltpu.VMEM((N_COL * 128, 128), F32),
            pltpu.VMEM((128, 128), F32),
            pltpu.VMEM((K, WIDTH), F32),
            pltpu.VMEM((K, WIDTH), F32),
            pltpu.VMEM((K, WIDTH), F32),
            pltpu.VMEM((K, K), F32),
            pltpu.VMEM((2, K, WIDTH), BF16),
            pltpu.VMEM((2, N_ROW, K, WIDTH), BF16),
            pltpu.VMEM((2, N_CHIP, 2, K, WIDTH), BF16),
            pltpu.VMEM((2, N_ROW, K, WIDTH), BF16),
            pltpu.VMEM((2, 2, N_CHIP, K, WIDTH), BF16),
            pltpu.VMEM((2, N_CHIP, K, WIDTH), BF16),
            pltpu.VMEM((2, N_CHIP, K, WIDTH), BF16),
            pltpu.VMEM((N_COL, K, WIDTH), BF16),
            pltpu.VMEM((2, N_ROW, K, WIDTH), BF16),
            pltpu.VMEM((2, N_CHIP, K, WIDTH), BF16),
            pltpu.VMEM((6, 8, 128), F32),
            pltpu.VMEM((3, N_ROW, 8, 128), F32),
            pltpu.VMEM((3, N_COL, 8, 128), F32),
            pltpu.SemaphoreType.DMA((6,)),
            pltpu.SemaphoreType.DMA((3,)),
            pltpu.SemaphoreType.DMA((SLOTS // 64, 4)),
            pltpu.SemaphoreType.DMA((kinds,)),
            pltpu.SemaphoreType.DMA((kinds,)),
            pltpu.SemaphoreType.DMA((2, N_ROW)),
            pltpu.SemaphoreType.DMA((2, N_COL)),
            pltpu.SemaphoreType.DMA((2, N_ROW)),
            pltpu.SemaphoreType.DMA((2, N_CHIP)),
            pltpu.SemaphoreType.DMA((2,)),
            pltpu.SemaphoreType.DMA((3,)),
            pltpu.SemaphoreType.DMA((3,)),
        ],
        compiler_params=pltpu.CompilerParams(
            collective_id=0, has_side_effects=True, vmem_limit_bytes=58 << 20
        ),
        cost_estimate=pl.CostEstimate(flops=1 << 30, bytes_accessed=9 << 20, transcendentals=0),
    )(block_x, tile_values, row_block, col_block, tile_counts)
    return pl.pallas_call(
        pass_results, out_shape=vectors, in_specs=[vmem] * 3, out_specs=(vmem,) * 3
    )(*results)


def solution(mesh):
    placed = (
        P(("row", "col"), None),
        P("row", "col", None, None),
        P("row", "col", None),
        P("row", "col", None),
        P("row", "col"),
    )
    return jax.shard_map(
        local,
        mesh=mesh,
        in_specs=placed,
        out_specs=(P(("row", "col"), None), P(("row", "col"), None), P()),
        check_vma=False,
    )
```

```python
import functools

import jax
import jax.numpy as jnp
from jax import lax
from jax.experimental import pallas as pl
from jax.experimental.pallas import tpu as pltpu
from jax.sharding import PartitionSpec as P

F32 = jnp.float32
BF16 = jnp.bfloat16
TILE = 64
K = 16
SEGB = 16
SLOTS = 1024
GROUPS = SLOTS // 4
WIDTH = K * TILE
N_ROW = 8
N_COL = 16
N_CHIP = N_COL // 2
RB = N_ROW * SEGB
CB = N_COL * SEGB
STAGE_PITCH = 136
Y_PITCH = 520
EARLY_CHUNKS = 3
HIGHEST = lax.Precision.HIGHEST
NT = (((1,), (1,)), ((), ()))
NN = (((1,), (0,)), ((), ()))


def left_half(rows):
    return lax.broadcasted_iota(jnp.int32, (rows, 128), 1) < TILE


def swap_halves(value):
    return pltpu.roll(value, TILE, 1)


def lane_block(index):
    start = index * 128
    if not isinstance(index, int):
        start = pl.multiple_of(start, 128)
    return pl.ds(start, 128)


def flat_to_by_vector(flat, temp, out):
    lt = left_half(8)

    def step(pair, carry):
        low = flat[0:8, lane_block(pair)]
        high = flat[8:16, lane_block(pair)]
        temp[pl.ds(2 * pair, 8, stride=K), :] = jnp.where(lt, low, swap_halves(high))
        temp[pl.ds(2 * pair + 1, 8, stride=K), :] = jnp.where(lt, swap_halves(low), high)
        return carry

    lax.fori_loop(0, K // 2, step, 0, unroll=True)
    gather_blocks(temp, out)


def gather_blocks(temp, out):
    def step(p, carry):
        out[:, lane_block(p)] = temp[pl.ds(pl.multiple_of(p * K, K), K), :]
        return carry

    lax.fori_loop(0, 8, step, 0, unroll=True)


def by_vector_to_by_row(by_vector, temp, out):
    def spread(p, carry):
        temp[pl.ds(pl.multiple_of(p * K, K), K), :] = by_vector[:, lane_block(p)]
        return carry

    def collect(k, carry):
        out[pl.ds(pl.multiple_of(k * 8, 8), 8), :] = temp[pl.ds(k, 8, stride=K), :]
        return carry

    lax.fori_loop(0, 8, spread, 0, unroll=True)
    lax.fori_loop(0, K, collect, 0, unroll=True)


def by_row_to_flat(by_row, flat):
    lt = left_half(8)

    def step(pair, carry):
        even = by_row[pl.ds(pl.multiple_of(pair * 16, 8), 8), :]
        odd = by_row[pl.ds(pl.multiple_of(pair * 16 + 8, 8), 8), :]
        flat[0:8, lane_block(pair)] = jnp.where(lt, even, swap_halves(odd))
        flat[8:16, lane_block(pair)] = jnp.where(lt, swap_halves(even), odd)
        return carry

    lax.fori_loop(0, K // 2, step, 0, unroll=True)


def load_groups(raw, stage, tiles, chunk, count):
    lt = left_half(16)
    lane_row = lax.broadcasted_iota(jnp.int32, (16, 128), 0)

    def half(a, carry):
        live = [lane_row + ((2 * a + b) * GROUPS + chunk * 16) < count for b in range(2)]

        def step(m, inner):
            first = jnp.where(live[0], raw[chunk, 2 * a, :, lane_block(m)].astype(F32), 0.0)
            second = jnp.where(live[1], raw[chunk, 2 * a + 1, :, lane_block(m)].astype(F32), 0.0)
            even = jnp.where(lt, first, swap_halves(second))
            odd = jnp.where(lt, swap_halves(first), second)
            for h in range(2):
                base = h * 8 * STAGE_PITCH + a * TILE + 2 * m
                stage[pl.ds(base, 8, stride=STAGE_PITCH), :] = even[h * 8 : h * 8 + 8]
                stage[pl.ds(base + 1, 8, stride=STAGE_PITCH), :] = odd[h * 8 : h * 8 + 8]
            return inner

        return lax.fori_loop(0, 32, step, carry, unroll=True)

    lax.fori_loop(0, 2, half, 0, unroll=True)

    def narrow(u, carry):
        tiles[chunk * 16 + u] = stage[pl.ds(pl.multiple_of(u * STAGE_PITCH, 8), 128), :].astype(BF16)
        return carry

    lax.fori_loop(0, 16, narrow, 0, unroll=True)


def fill_table(own, table, base):
    lt = left_half(16)
    zero = jnp.zeros((16, 128), BF16)

    def step(p, carry):
        both = own[:, lane_block(p)]
        turned = swap_halves(both)
        table[base + p, 0] = jnp.where(lt, both, zero)
        table[base + p, 1] = jnp.where(lt, zero, turned)
        table[base + 8 + p, 0] = jnp.where(lt, turned, zero)
        table[base + 8 + p, 1] = jnp.where(lt, zero, both)
        return carry

    lax.fori_loop(0, 8, step, 0, unroll=True)


def multiply(index, table, tiles, products, forward, turned=None):
    lt = left_half(16)

    def step(q, carry):
        picked = [table[index[0, 0, g * GROUPS + q], (g % 2) if forward else (g // 2)] for g in range(4)]
        left = jnp.concatenate(picked, axis=0)
        matrix = tiles[q]
        if turned is not None:
            turned[q] = matrix.T
        out = lax.dot_general(left, matrix, NN, preferred_element_type=F32)
        for s in range(2):
            one, two = (s, 2 + s) if forward else (2 * s, 2 * s + 1)
            merged = jnp.where(lt, out[one * 16 : one * 16 + 16], out[two * 16 : two * 16 + 16])
            place = s * GROUPS + q
            products[pl.ds(place, 8, stride=Y_PITCH), :] = merged[:8]
            products[pl.ds(8 * Y_PITCH + place, 8, stride=Y_PITCH), :] = merged[8:]
        return carry

    lax.fori_loop(0, GROUPS, step, 0, unroll=True)


def add_up(places, products, temp, blocks):
    lt = left_half(8)
    targets = blocks // SEGB

    def step(pair, carry):
        part = [
            products[pl.ds(pl.multiple_of((2 * pair + i) * Y_PITCH, 8), SLOTS // 2), :].astype(BF16) for i in range(2)
        ]
        total = jnp.dot(places[...], jnp.concatenate(part, axis=1), preferred_element_type=F32)
        for target in range(targets):
            for i in range(2):
                half = []
                for h in range(2):
                    first = target * SEGB + h * 8
                    left = total[first : first + 8, i * 128 : i * 128 + 128]
                    right = total[blocks + first : blocks + first + 8, i * 128 : i * 128 + 128]
                    both = jnp.where(lt, left, right)
                    half.append(both + swap_halves(both))
                temp[pl.ds(target * 128 + 2 * pair + i, 8, stride=K), :] = jnp.where(lt, half[0], half[1])
        return carry

    lax.fori_loop(0, K // 2, step, 0, unroll=True)


def narrow_sums(temp, first, stride, out, count):
    def step(target, carry):
        for p in range(8):
            start = (first + target * stride) * 128 + p * K
            out[target, :, p * 128 : p * 128 + 128] = temp[pl.ds(pl.multiple_of(start, K), K), :].astype(BF16)
        return carry

    lax.fori_loop(0, count, step, 0, unroll=True)


def add_pair(temp, first, other, out, count):
    def step(target, carry):
        for p in range(8):
            start = (first + target * 2) * 128 + p * K
            here = temp[pl.ds(pl.multiple_of(start, K), K), :]
            lanes = slice(p * 128, p * 128 + 128)
            out[target, :, lanes] = (here + other[target, :, lanes].astype(F32)).astype(BF16)
        return carry

    lax.fori_loop(0, count, step, 0, unroll=True)


def factor(norm):
    row = lax.broadcasted_iota(jnp.int32, (K, K), 0)
    lane = lax.broadcasted_iota(jnp.int32, (K, K), 1)

    def step(j, carry):
        matrix, inverse = carry
        pivot_row = jnp.sum(jnp.where(row == j, matrix, 0.0), axis=0, keepdims=True)
        pivot_inv = jnp.sum(jnp.where(row == j, inverse, 0.0), axis=0, keepdims=True)
        column = jnp.sum(jnp.where(lane == j, matrix, 0.0), axis=1, keepdims=True)
        pivot = jnp.sum(jnp.where((lane == j) & (row == j), matrix, 0.0), keepdims=True)
        scale = jnp.where(row[:, 0:1] > j, column / pivot, 0.0)
        return matrix - scale * pivot_row, inverse - scale * pivot_inv

    start = (norm, jnp.where(row == lane, 1.0, 0.0).astype(F32))
    matrix, inverse = lax.fori_loop(0, K, step, start)
    diagonal = jnp.sum(jnp.where(row == lane, matrix, 0.0), axis=1, keepdims=True)
    return inverse, 1.0 / diagonal


def kernel(
    block_x, tile_values, row_block, col_block, tile_counts,
    residual_out, image_out, gram_out,
    raw, stage, tiles, turned, table_r, table_c, place_r, place_c, prod_r, prod_c,
    flat_x, row_s, col_s, count_s, row_v, col_v, temp, by_row, vec_x, vec_a, vec_b, gram_last, own, got_r, got_c, part_r, part_c, pair_c, both_c, spare, sum_r, sum_c, gram_own, gram_r, gram_c,
    enter_sem, leave_sem, load_sem, send_r, send_c, recv_r, recv_c, recv_sum_r, recv_sum_c, pair_sem, gram_recv_r, gram_recv_c,
):
    my_row, my_col = lax.axis_index("row"), lax.axis_index("col")
    my_chip, my_core = my_col // 2, lax.rem(my_col, 2)
    sibling = my_chip * 2 + 1 - my_core

    def send(axis, peer, source, target, sent, arrived):
        pltpu.make_async_remote_copy(
            src_ref=source, dst_ref=target, send_sem=sent, recv_sem=arrived,
            device_id={axis: peer}, device_id_type=pl.DeviceIdType.MESH,
        ).start()

    def others(size, me, use):
        def step(d, carry):
            use(lax.rem(me + d, size))
            return carry

        lax.fori_loop(1, size, step, 0, unroll=True)

    def wait_bytes(block, sem):
        pltpu.make_async_copy(block, block, sem).wait()

    def load(chunk, g):
        return pltpu.make_async_copy(
            tile_values.at[0, 0, pl.ds(pl.multiple_of(g * GROUPS + chunk * 16, 16), 16), :],
            raw.at[chunk, g], load_sem.at[chunk, g],
        )

    def start_load(chunk, carry):
        for g in range(4):
            load(chunk, g).start()
        return carry

    barrier = pltpu.get_barrier_semaphore()

    def greet(axis, peer):
        pl.semaphore_signal(barrier, inc=1, device_id={axis: peer}, device_id_type=pl.DeviceIdType.MESH)

    others(N_ROW, my_row, lambda peer: greet("row", peer))
    others(N_COL, my_col, lambda peer: greet("col", peer))

    def put_gram(which, value):
        gram_own[which] = jnp.zeros((8, 128), F32)
        gram_own[which, :, 0:K] = value[0:8]
        gram_own[which, :, K : 2 * K] = value[8:16]

    pairs = (
        (block_x, flat_x), (tile_counts, count_s), (row_block, row_s), (col_block, col_s),
        (row_block, row_v), (col_block, col_v),
    )
    enter = [pltpu.make_async_copy(a, b, enter_sem.at[i]) for i, (a, b) in enumerate(pairs)]

    def leave(which, source, target):
        return pltpu.make_async_copy(source, target, leave_sem.at[which])

    for arrival in enter:
        arrival.start()
    lax.fori_loop(0, SLOTS // 64, start_load, 0)
    enter[0].wait()
    flat_to_by_vector(flat_x, temp, vec_x)
    own[0] = vec_x[...].astype(BF16)
    norm = lax.dot_general(vec_x[...], vec_x[...], NT, precision=HIGHEST, preferred_element_type=F32)
    put_gram(0, norm)
    enter[1].wait()
    count = count_s[0, 0]

    def arrange(chunk, carry):
        for g in range(4):
            load(chunk, g).wait()
        load_groups(raw, stage, tiles, chunk, count)
        return carry

    for arrival in enter[2:]:
        arrival.wait()
    for s in range(2):
        columns = jnp.concatenate(
            [col_v[0, :, s * 256 : s * 256 + 256], col_v[0, :, 512 + s * 256 : 768 + s * 256]], axis=1
        )
        hit = lax.broadcasted_iota(jnp.int32, (CB, 512), 0) == columns
        place_c[s * CB : s * CB + CB, :] = jnp.where(hit, 1.0, 0.0).astype(BF16)
        hit = lax.broadcasted_iota(jnp.int32, (RB, 512), 0) == row_v[0, :, s * 512 : s * 512 + 512]
        place_r[s * RB : s * RB + RB, :] = jnp.where(hit, 1.0, 0.0).astype(BF16)
    lax.fori_loop(0, EARLY_CHUNKS, arrange, 0)
    pl.semaphore_wait(barrier, N_ROW + N_COL - 2)

    def gather(step, beside):
        def to_row(peer):
            send("row", peer, own.at[step], got_r.at[step, my_row], send_r.at[step], recv_r.at[step, my_row])

        def to_col(peer):
            send(
                "col", peer, own.at[step], got_c.at[step, my_chip, my_core], send_c.at[step], recv_c.at[step, my_col]
            )

        others(N_ROW, my_row, to_row)
        others(N_CHIP, my_chip, lambda chip: to_col(chip * 2 + my_core))
        to_col(sibling)
        got_c[step, my_chip, my_core] = own[step]
        beside()

    def forward(step):
        def pass_on(chip):
            slot = chip * 2 + my_core
            block = got_c.at[step, chip, my_core]
            wait_bytes(block, recv_c.at[step, slot])
            send("col", sibling, block, block, send_c.at[step], recv_c.at[step, slot])

        others(N_CHIP, my_chip, pass_on)

    def gram_row(which):
        def to_row(peer):
            send(
                "row", peer, gram_own.at[which], gram_r.at[which, my_row], send_r.at[4 + which], gram_recv_r.at[which]
            )

        others(N_ROW, my_row, to_row)
        gram_r[which, my_row] = gram_own[which]

    def gram_col(which):
        wait_bytes(gram_r.at[which, pl.ds(0, N_ROW - 1)], gram_recv_r.at[which])
        gram_own[3 + which] = jnp.sum(gram_r[which], axis=0)

        def to_col(peer):
            send(
                "col", peer, gram_own.at[3 + which], gram_c.at[which, my_col], send_c.at[4 + which],
                gram_recv_c.at[which],
            )

        others(N_COL, my_col, to_col)
        gram_c[which, my_col] = gram_own[3 + which]

    def gram_done(which):
        wait_bytes(gram_c.at[which, pl.ds(0, N_COL - 1)], gram_recv_c.at[which])
        total = jnp.sum(gram_c[which], axis=0)
        return jnp.concatenate([total[:, 0:K], total[:, K : 2 * K]], axis=0)

    def cross_part(step):
        total = jnp.zeros((K, K), F32)
        for side in range(2):
            core = my_core if side == 0 else 1 - my_core
            sums = part_c[step, side].reshape(N_CHIP * K, WIDTH)
            vectors = got_c[step, :, core].reshape(N_CHIP * K, WIDTH)
            pairs = lax.dot_general(sums, vectors, NT, preferred_element_type=F32)
            for chip in range(N_CHIP):
                total += pairs[chip * K : chip * K + K, chip * K : chip * K + K]
        return total

    def fill_all(step):
        def enter(chip, carry):
            for core in range(2):
                fill_table(got_c.at[step, chip, core], table_c, (chip * 2 + core) * SEGB)
            return carry

        lax.fori_loop(0, N_CHIP, enter, 0, unroll=4)

    def finish_sends(step):
        sent_c = spare.at[pl.ds(0, N_COL - 1)]
        wait_bytes(got_r.at[step, pl.ds(0, N_ROW - 1)], send_r.at[step])
        wait_bytes(sent_c, send_c.at[step])
        wait_bytes(got_r.at[step, pl.ds(0, N_ROW - 1)], send_r.at[2 + step])
        wait_bytes(sent_c, send_c.at[2 + step])
        for which in (0, 1) if step == 0 else (2,):
            wait_bytes(gram_r.at[which, pl.ds(0, N_ROW - 1)], send_r.at[4 + which])
            wait_bytes(gram_c.at[which, pl.ds(0, N_COL - 1)], send_c.at[4 + which])

    def arrange_rest():
        gram_row(0)
        lax.fori_loop(EARLY_CHUNKS, SLOTS // 64, arrange, 0)

    gather(0, arrange_rest)
    gram_col(0)

    def product(step):
        def arrive_row(peer):
            wait_bytes(got_r.at[step, peer], recv_r.at[step, peer])

        def enter_row(d, carry):
            peer = lax.rem(my_row + d, N_ROW)
            fill_table(got_r.at[step, peer], table_r, peer * SEGB)
            return carry

        def arrive_other(chip):
            wait_bytes(got_c.at[step, chip, 1 - my_core], recv_c.at[step, chip * 2 + 1 - my_core])

        fill_table(own.at[step], table_r, my_row * SEGB)
        others(N_ROW, my_row, arrive_row)
        lax.fori_loop(1, N_ROW, enter_row, 0, unroll=True)
        multiply(row_s, table_r, tiles, prod_c, False, turned if step == 0 else None)
        forward(step)
        add_up(place_c, prod_c, temp, CB)
        narrow_sums(temp, 1 - my_core, 2, part_c.at[step, 1], N_CHIP)
        send("col", sibling, part_c.at[step, 1], pair_c.at[step], send_c.at[2 + step], pair_sem.at[step])
        narrow_sums(temp, my_core, 2, part_c.at[step, 0], N_CHIP)
        arrive_other(my_chip)
        others(N_CHIP, my_chip, arrive_other)
        put_gram(1 + step, cross_part(step))
        gram_row(1 + step)
        fill_all(step)
        wait_bytes(pair_c.at[step], pair_sem.at[step])
        add_pair(temp, my_core, pair_c.at[step], both_c.at[step], N_CHIP)

        def sums_to_col(chip):
            send(
                "col", chip * 2 + my_core, both_c.at[step, chip], sum_c.at[step, my_chip], send_c.at[2 + step],
                recv_sum_c.at[step, my_chip],
            )

        others(N_CHIP, my_chip, sums_to_col)
        multiply(col_s, table_c, turned, prod_r, True)
        gram_col(1 + step)
        add_up(place_r, prod_r, temp, RB)
        narrow_sums(temp, 0, 1, part_r.at[step], N_ROW)

        def sums_to_row(peer):
            send(
                "row", peer, part_r.at[step, peer], sum_r.at[step, my_row], send_r.at[2 + step],
                recv_sum_r.at[step, my_row],
            )

        others(N_ROW, my_row, sums_to_row)
        if step == 0:
            inverse, scale = factor(gram_done(0))
            norm_inverse = lax.dot_general(
                inverse * scale, inverse, (((0,), (0,)), ((), ())), precision=HIGHEST, preferred_element_type=F32
            )

        def add_col(chip):
            wait_bytes(sum_c.at[step, chip], recv_sum_c.at[step, chip])
            vec_a[...] += sum_c[step, chip].astype(F32)

        vec_a[...] = both_c[step, my_chip].astype(F32) + part_r[step, my_row].astype(F32)
        others(N_CHIP, my_chip, add_col)
        half = gram_done(1 + step)
        cross = half + half.T
        if step == 0:
            coupling = jnp.dot(cross, norm_inverse, precision=HIGHEST, preferred_element_type=F32)
            vec_a[...] -= jnp.dot(coupling, vec_x[...], precision=HIGHEST, preferred_element_type=F32)

        def arrive_sum(peer):
            wait_bytes(sum_r.at[step, peer], recv_sum_r.at[step, peer])

        others(N_ROW, my_row, arrive_sum)
        sum_r[step, my_row] = jnp.zeros((K, WIDTH), BF16)

        def add_row(p, carry):
            total = vec_a[:, lane_block(p)]
            for slot in range(N_ROW):
                total += sum_r[step, slot, :, lane_block(p)].astype(F32)
            vec_a[:, lane_block(p)] = total
            if step == 0:
                own[1, :, lane_block(p)] = total.astype(BF16)
            return carry

        lax.fori_loop(0, 8, add_row, 0, unroll=True)
        return cross

    product(0)

    def keep_residual():
        by_vector_to_by_row(vec_a, temp, by_row)
        by_row_to_flat(by_row, vec_x)
        leave(0, vec_x, residual_out).start()
        finish_sends(0)

    gather(1, keep_residual)
    last = product(1)
    by_vector_to_by_row(vec_a, temp, by_row)
    by_row_to_flat(by_row, vec_b)
    gram_last[...] = last * (1.0 / (N_ROW * N_COL * SEGB * TILE))
    leave(1, vec_b, image_out).start()
    leave(2, gram_last, gram_out).start()
    finish_sends(1)
    leave(0, vec_x, residual_out).wait()
    leave(1, vec_b, image_out).wait()
    leave(2, gram_last, gram_out).wait()


def pass_results(residual, image, gram, residual_out, image_out, gram_out):
    residual_out[...] = residual[...]
    image_out[...] = image[...]
    gram_out[...] = gram[...]


def local(block_x, tile_values, row_block, col_block, tile_counts):
    vmem = pl.BlockSpec(memory_space=pltpu.VMEM)
    anywhere = pl.BlockSpec(memory_space=pl.ANY)
    kinds = 7
    vectors = (
        jax.ShapeDtypeStruct((SEGB, WIDTH), F32),
        jax.ShapeDtypeStruct((SEGB, WIDTH), F32),
        jax.ShapeDtypeStruct((K, K), F32),
    )
    results = pl.pallas_call(
        kernel,
        out_shape=vectors,
        in_specs=[anywhere] * 5,
        out_specs=(anywhere,) * 3,
        scratch_shapes=[
            pltpu.VMEM((SLOTS // 64, 4, 16, TILE * TILE), BF16),
            pltpu.VMEM((16 * STAGE_PITCH, 128), F32),
            pltpu.VMEM((GROUPS, 128, 128), BF16),
            pltpu.VMEM((GROUPS, 128, 128), BF16),
            pltpu.VMEM((RB, 2, K, 128), BF16),
            pltpu.VMEM((CB, 2, K, 128), BF16),
            pltpu.VMEM((2 * RB, 512), BF16),
            pltpu.VMEM((2 * CB, 512), BF16),
            pltpu.VMEM((K * Y_PITCH, 128), F32),
            pltpu.VMEM((K * Y_PITCH, 128), F32),
            pltpu.VMEM((SEGB, WIDTH), F32),
            pltpu.SMEM((1, 1, SLOTS), jnp.int32),
            pltpu.SMEM((1, 1, SLOTS), jnp.int32),
            pltpu.SMEM((1, 1), jnp.int32),
            pltpu.VMEM((1, 1, SLOTS), jnp.int32),
            pltpu.VMEM((1, 1, SLOTS), jnp.int32),
            pltpu.VMEM((N_COL * 128, 128), F32),
            pltpu.VMEM((128, 128), F32),
            pltpu.VMEM((K, WIDTH), F32),
            pltpu.VMEM((K, WIDTH), F32),
            pltpu.VMEM((K, WIDTH), F32),
            pltpu.VMEM((K, K), F32),
            pltpu.VMEM((2, K, WIDTH), BF16),
            pltpu.VMEM((2, N_ROW, K, WIDTH), BF16),
            pltpu.VMEM((2, N_CHIP, 2, K, WIDTH), BF16),
            pltpu.VMEM((2, N_ROW, K, WIDTH), BF16),
            pltpu.VMEM((2, 2, N_CHIP, K, WIDTH), BF16),
            pltpu.VMEM((2, N_CHIP, K, WIDTH), BF16),
            pltpu.VMEM((2, N_CHIP, K, WIDTH), BF16),
            pltpu.VMEM((N_COL, K, WIDTH), BF16),
            pltpu.VMEM((2, N_ROW, K, WIDTH), BF16),
            pltpu.VMEM((2, N_CHIP, K, WIDTH), BF16),
            pltpu.VMEM((6, 8, 128), F32),
            pltpu.VMEM((3, N_ROW, 8, 128), F32),
            pltpu.VMEM((3, N_COL, 8, 128), F32),
            pltpu.SemaphoreType.DMA((6,)),
            pltpu.SemaphoreType.DMA((3,)),
            pltpu.SemaphoreType.DMA((SLOTS // 64, 4)),
            pltpu.SemaphoreType.DMA((kinds,)),
            pltpu.SemaphoreType.DMA((kinds,)),
            pltpu.SemaphoreType.DMA((2, N_ROW)),
            pltpu.SemaphoreType.DMA((2, N_COL)),
            pltpu.SemaphoreType.DMA((2, N_ROW)),
            pltpu.SemaphoreType.DMA((2, N_CHIP)),
            pltpu.SemaphoreType.DMA((2,)),
            pltpu.SemaphoreType.DMA((3,)),
            pltpu.SemaphoreType.DMA((3,)),
        ],
        compiler_params=pltpu.CompilerParams(
            collective_id=0, has_side_effects=True, vmem_limit_bytes=58 << 20
        ),
        cost_estimate=pl.CostEstimate(flops=1 << 30, bytes_accessed=9 << 20, transcendentals=0),
    )(block_x, tile_values, row_block, col_block, tile_counts)
    return pl.pallas_call(
        pass_results, out_shape=vectors, in_specs=[vmem] * 3, out_specs=(vmem,) * 3
    )(*results)


def solution(mesh):
    placed = (
        P(("row", "col"), None),
        P("row", "col", None, None),
        P("row", "col", None),
        P("row", "col", None),
        P("row", "col"),
    )
    return jax.shard_map(
        local,
        mesh=mesh,
        in_specs=placed,
        out_specs=(P(("row", "col"), None), P(("row", "col"), None), P()),
        check_vma=False,
    )
```
